32 devices in a mesh: grp: 2 (over y), section: 4 (over x, core), seg: 4 (over z).
Axes of the slice: x: 2, y: 2, z: 4, core: 2. Of those that a mesh axis runs over, the one named last changes fastest.
Arguments:
- inputs: bfloat16 [4, 8, 256, 2048], P('section', ('grp', 'seg')), parts along dimension 1, may hold values from -44 to 44
- memory: bfloat16 [4, 8, 32, 2048], P('section', ('grp', 'seg')), parts along dimension 1, may hold values from -6 to 6
- out_cot: bfloat16 [4, 8, 288, 2048], P('section', ('grp', 'seg')), parts along dimension 1, may hold values from -6 to 6
- head_cot: bfloat16 [4, 8, 288, 2048], P('section', ('grp', 'seg')), parts along dimension 1, may hold values from -6 to 6
- w_query: bfloat16 [4, 2048, 2048], P('section', 'seg'), may hold values from -0.61871843 to 0.61871843
- w_key: bfloat16 [4, 2048, 512], P('section', 'seg'), may hold values from -0.61871843 to 0.61871843
- w_value: bfloat16 [4, 2048, 512], P('section', 'seg'), may hold values from -0.125 to 0.125
- gain: bfloat16 [4, 2048], P('section'), may hold values from 0.5 to 1.5
Outputs:
- token_cot_below: bfloat16 [4, 8, 256, 2048], P('section', ('grp', 'seg')), parts along dimension 1
- memory_cot_before: bfloat16 [4, 8, 32, 2048], P('section', ('grp', 'seg')), parts along dimension 1
- grad_query: float32 [8, 2048, 2048], P(('grp', 'section'), 'seg'), parts along dimension 0
- grad_key: float32 [8, 2048, 512], P(('grp', 'section'), 'seg'), parts along dimension 0
- grad_value: float32 [8, 2048, 512], P(('grp', 'section'), 'seg'), parts along dimension 0
- grad_gain: float32 [8, 2048], P(('grp', 'section'), 'seg'), parts along dimension 0
The draws below stay inside these ranges and needn't reach their ends.
There are 2 independent parts, one for each index of `grp`. The reference program is written for one: setup_inputs(seed, part) draws one part's arguments, and reference() takes and returns one part's arrays. A program takes and returns all parts, laid end to end along the dimension named above; an argument that names none is the same for every part. Nothing has to cross between parts.
All inputs are finite; a program needn't handle non-finite values.
Results may differ from the reference program's by a relative error of at most 0.01.
The reference program's roundings to bfloat16 on the way (of `rows`, `normed`, `probs_b` and `d_scores`) count: a program that leaves them out, or rounds other values in their place, can miss the bound.
Values may be sent and summed in bfloat16 or wider, within the bound.
No kernel may reach another device: no remote copies, remote signals or barrier semaphores. Data moves between devices by JAX's collectives and lax.ppermute only.
A program may use at most 128 MiB of HBM per device.

```python
import math
import jax
import jax.numpy as jnp
from jax import lax

D = 2048
HEADS = 4
GROUP = 4
HD = 128
MEM = 32
SEG = 256
QW = 2048
KW = 512
OUTROWS = 288
LAYERS = 4
SEGMENTS = 4


def projection(key, number, repeats):
    own_key = jax.random.fold_in(key, number)
    own = jnp.clip(jax.random.normal(own_key, (LAYERS, D, HEADS, repeats, HD), jnp.float32), -4.0, 4.0) / math.sqrt(D)
    return own.reshape(LAYERS, D, HEADS * repeats * HD).astype(jnp.bfloat16)


def draw_w_query(key, part):
    return projection(key, 1, GROUP)


def draw_w_key(key, part):
    return projection(key, 2, 1)


def draw_inputs(key, part):
    key = jax.random.fold_in(key, 3)
    keys = jax.random.split(key, 1)
    shape = (LAYERS, SEGMENTS, SEG, D)
    value = jnp.clip(jax.random.normal(keys[0], shape, jnp.float32), -6.0, 6.0)
    return value.astype(jnp.bfloat16)


def levels(key, dims, cuts, low, top_value):
    def one(dim, blocks):
        heights = jax.random.uniform(jax.random.fold_in(jax.random.fold_in(key, 6), dim), (blocks,), jnp.float32, low / len(cuts), top_value / len(cuts))
        return jnp.repeat(jnp.exp(heights), dims[dim] // blocks).reshape((-1,) + (1,) * (len(dims) - dim - 1))

    loudness = one(*cuts[0])
    for cut in cuts[1:]:
        loudness = loudness * one(*cut)
    return loudness


def gaussian(key, dims, width, most, cuts=(), dtype=jnp.bfloat16):
    loudness = levels(key, dims, cuts, -0.22, 0.18) if cuts else 1.0
    entries = jax.random.normal(key, dims, jnp.float32) * width * loudness
    return jnp.minimum(jnp.maximum(entries, -most), most).astype(dtype)


def setup_inputs(seed: int = 0, part: int = 0) -> dict:
    key_of = jax.random.split(jax.random.key(seed), 9)
    own_keys = jax.random.split(jax.random.fold_in(key_of[8], part), 9)
    inputs = draw_inputs(jax.random.fold_in(jax.random.fold_in(key_of[8], part), 71), part)
    memory = gaussian(own_keys[1], (LAYERS, SEGMENTS, MEM, D), 1.0, 6.0, ((0, 4), (1, 4)))
    out_cot = gaussian(own_keys[2], (LAYERS, SEGMENTS, OUTROWS, D), 1.0, 6.0, ((0, 4), (1, 4)))
    head_cot = gaussian(own_keys[3], (LAYERS, SEGMENTS, OUTROWS, QW), 1.0, 6.0, ((0, 4), (1, 4)))
    w_query = draw_w_query(jax.random.fold_in(key_of[8], 71), part)
    w_key = draw_w_key(jax.random.fold_in(key_of[8], 71), part)
    w_value = gaussian(key_of[6], (LAYERS, D, KW), D ** -0.5, 0.125, ((0, 4), (1, 4)))
    gain = jnp.clip(1.0 + 0.1 * jax.random.normal(key_of[7], (LAYERS, D), jnp.float32), 0.5, 1.5).astype(jnp.bfloat16)
    return {"inputs": inputs, "memory": memory, "out_cot": out_cot, "head_cot": head_cot, "w_query": w_query, "w_key": w_key, "w_value": w_value, "gain": gain}


def cell(x, mem, ocot, hcot, wq, wk, wv, g):
    rows = jnp.concatenate([mem, x, mem], 0)
    total = rows.shape[0]
    zf = rows.astype(jnp.float32)
    inv = lax.rsqrt(lax.optimization_barrier(jnp.mean(zf * zf, -1, keepdims=True)) + 1e-05)
    unit = zf * inv
    gain_f = g.astype(jnp.float32)
    normed = (unit * gain_f).astype(jnp.bfloat16)
    query = jnp.dot(normed, wq, preferred_element_type=jnp.float32).astype(jnp.bfloat16).reshape(total, HEADS, GROUP, HD)
    keys = jnp.dot(normed, wk, preferred_element_type=jnp.float32).astype(jnp.bfloat16).reshape(total, HEADS, HD)
    values = jnp.dot(normed, wv, preferred_element_type=jnp.float32).astype(jnp.bfloat16).reshape(total, HEADS, HD)
    scale = HD ** (-0.5)
    scores = jnp.einsum('qhgd,khd->hgqk', query.astype(jnp.float32), keys.astype(jnp.float32)) * scale
    places = jnp.arange(total)
    causal = places[:, None] >= places[None, :]
    scores = jnp.where(causal[None, None], scores, -1e+30)
    probs = jax.nn.softmax(scores, -1)
    probs_b = probs.astype(jnp.bfloat16)
    mem_len = mem.shape[0]
    cot = jnp.concatenate([jnp.zeros((mem_len, ocot.shape[1]), jnp.bfloat16), ocot], 0)
    d_attn = jnp.concatenate([jnp.zeros((mem_len, hcot.shape[1]), jnp.bfloat16), hcot], 0)
    d_heads = d_attn.reshape(total, HEADS, GROUP, HD).astype(jnp.float32)
    d_probs = jnp.einsum('qhgd,khd->hgqk', d_heads, values.astype(jnp.float32))
    d_scores = (probs * (d_probs - lax.optimization_barrier(jnp.sum(probs * d_probs, -1, keepdims=True))) * scale).astype(jnp.bfloat16)
    d_values = jnp.einsum('hgqk,qhgd->khd', probs_b.astype(jnp.float32), d_heads).astype(jnp.bfloat16).reshape(total, HEADS * HD)
    d_query = jnp.einsum('hgqk,khd->qhgd', d_scores.astype(jnp.float32), keys.astype(jnp.float32)).astype(jnp.bfloat16).reshape(total, HEADS * GROUP * HD)
    d_keys = jnp.einsum('hgqk,qhgd->khd', d_scores.astype(jnp.float32), query.astype(jnp.float32)).astype(jnp.bfloat16).reshape(total, HEADS * HD)
    part_q = jnp.dot(normed.T, d_query, preferred_element_type=jnp.float32).astype(jnp.bfloat16)
    part_k = jnp.dot(normed.T, d_keys, preferred_element_type=jnp.float32).astype(jnp.bfloat16)
    part_v = jnp.dot(normed.T, d_values, preferred_element_type=jnp.float32).astype(jnp.bfloat16)
    part_q, part_k, part_v = lax.optimization_barrier((part_q, part_k, part_v))
    d_normed = jnp.dot(d_query, wq.T, preferred_element_type=jnp.float32)
    d_normed = d_normed + jnp.dot(d_keys, wk.T, preferred_element_type=jnp.float32)
    d_normed = d_normed + jnp.dot(d_values, wv.T, preferred_element_type=jnp.float32)
    grad_g = lax.optimization_barrier(jnp.sum(d_normed * unit, 0))
    d_unit = d_normed * gain_f
    d_rows = cot.astype(jnp.float32) + inv * (d_unit - unit * lax.optimization_barrier(jnp.mean(d_unit * unit, -1, keepdims=True)))
    seg_len = x.shape[0]
    token_part = d_rows[mem_len:mem_len + seg_len].astype(jnp.bfloat16)
    memory_part = (d_rows[:mem_len] + d_rows[mem_len + seg_len:]).astype(jnp.bfloat16)
    return (part_q, part_k, part_v, grad_g, token_part, memory_part)

def reference(inputs, memory, out_cot, head_cot, w_query, w_key, w_value, gain):

    def layer(packed):
        x_l, m_l, o_l, h_l, wq, wk, wv, g = packed

        def step(carry, pieces):
            x, m, o, h = pieces
            result = cell(x, m, o, h, wq, wk, wv, g)
            summed = tuple((a + b.astype(jnp.float32) for a, b in zip(carry, result[:4])))
            return (summed, (result[4], result[5]))
        start = (jnp.zeros((D, QW), jnp.float32), jnp.zeros((D, KW), jnp.float32), jnp.zeros((D, KW), jnp.float32), jnp.zeros((D,), jnp.float32))
        sums, parts = lax.scan(step, start, (x_l, m_l, o_l, h_l))
        return sums + parts
    outcome = lax.map(layer, (inputs, memory, out_cot, head_cot, w_query, w_key, w_value, gain))
    grad_query, grad_key, grad_value, grad_gain, token_part, memory_part = outcome
    token_cot_below = jnp.concatenate([token_part[1:], jnp.zeros_like(token_part[:1])], 0)
    memory_cot_before = jnp.concatenate([memory_part[:, 1:], jnp.zeros_like(memory_part[:, :1])], 1)
    return (token_cot_below, memory_cot_before, grad_query, grad_key, grad_value, grad_gain)
```

```python
import functools

import jax
import jax.numpy as jnp
from jax import lax
from jax.experimental import pallas as pl
from jax.experimental.pallas import tpu as pltpu
from jax.sharding import PartitionSpec as P

HEADS = 4
GROUP = 4
HD = 128
MIB = 1024 * 1024


def from_behind(block, axis, distance):
    devices = range(lax.axis_size(axis))
    route = [(i - distance, i) for i in devices if i - distance in devices]
    return lax.ppermute(block, axis, route)


def times_t(left, right):
    return lax.dot_general(
        left, right, (((1,), (1,)), ((), ())), preferred_element_type=jnp.float32
    )


def inner_rows(left, right):
    return lax.dot_general(
        left, right, (((0,), (0,)), ((), ())), preferred_element_type=jnp.float32
    )


def deliver(token_part, memory_part):
    below = from_behind(token_part, "section", -1)
    before = from_behind(memory_part, "seg", -1)
    return (below, before)


def on_device(inputs, memory, out_cot, head_cot, w_query, w_key, w_value, gain):
    whole_q, whole_k, whole_v = (
        lax.all_gather(w_query, "seg", axis=1, tiled=True),
        lax.all_gather(w_key, "seg", axis=1, tiled=True),
        lax.all_gather(w_value, "seg", axis=1, tiled=True),
    )
    wq = whole_q[0]
    wk = whole_k[0]
    wv = whole_v[0]
    tokens_in = inputs[0, 0]
    mem = memory[0, 0]
    ocot = out_cot[0, 0]
    hcot = head_cot[0, 0]
    gain_f = gain[0].astype(jnp.float32)
    mem_len = mem.shape[0]
    seg_len = tokens_in.shape[0]
    width = tokens_in.shape[1]
    query_width = wq.shape[1]
    rows = jnp.concatenate([mem, tokens_in, mem], 0)
    total = rows.shape[0]
    zf = rows.astype(jnp.float32)
    inv = lax.rsqrt(jnp.mean(zf * zf, -1, keepdims=True) + 1e-05)
    unit = zf * inv
    normed = (unit * gain_f).astype(jnp.bfloat16)
    query = (
        jnp.dot(normed, wq, preferred_element_type=jnp.float32)
        .astype(jnp.bfloat16)
        .reshape(total, HEADS, GROUP, HD)
    )
    keys = (
        jnp.dot(normed, wk, preferred_element_type=jnp.float32)
        .astype(jnp.bfloat16)
        .reshape(total, HEADS, HD)
    )
    values = (
        jnp.dot(normed, wv, preferred_element_type=jnp.float32)
        .astype(jnp.bfloat16)
        .reshape(total, HEADS, HD)
    )
    scale = HD ** (-0.5)
    scores = jnp.einsum("qhgd,khd->hgqk", query, keys, preferred_element_type=jnp.float32) * scale
    places = jnp.arange(total)
    causal = places[:, None] >= places[None, :]
    scores = jnp.where(causal[None, None], scores, -1e30)
    probs = jax.nn.softmax(scores, -1)
    probs_b = probs.astype(jnp.bfloat16)
    cot = jnp.concatenate([jnp.zeros((mem_len, width), jnp.bfloat16), ocot], 0)
    d_attn = jnp.concatenate([jnp.zeros((mem_len, query_width), jnp.bfloat16), hcot], 0)
    d_heads = d_attn.reshape(total, HEADS, GROUP, HD)
    d_probs = jnp.einsum("qhgd,khd->hgqk", d_heads, values, preferred_element_type=jnp.float32)
    d_scores = (probs * (d_probs - jnp.sum(probs * d_probs, -1, keepdims=True)) * scale).astype(
        jnp.bfloat16
    )
    d_values = jnp.einsum("hgqk,qhgd->khd", probs_b, d_heads, preferred_element_type=jnp.float32)
    d_values = d_values.astype(jnp.bfloat16).reshape(total, HEADS * HD)
    d_query = jnp.einsum("hgqk,khd->qhgd", d_scores, keys, preferred_element_type=jnp.float32)
    d_query = d_query.astype(jnp.bfloat16).reshape(total, query_width)
    d_keys = jnp.einsum("hgqk,qhgd->khd", d_scores, query, preferred_element_type=jnp.float32)
    d_keys = d_keys.astype(jnp.bfloat16).reshape(total, HEADS * HD)
    d_normed = times_t(d_query, wq) + times_t(d_keys, wk) + times_t(d_values, wv)
    grad_g = jnp.sum(d_normed * unit, 0)
    d_unit = d_normed * gain_f
    d_rows = cot.astype(jnp.float32) + inv * (
        d_unit - unit * jnp.mean(d_unit * unit, -1, keepdims=True)
    )
    token_part = d_rows[mem_len : mem_len + seg_len].astype(jnp.bfloat16)
    memory_part = (d_rows[:mem_len] + d_rows[mem_len + seg_len :]).astype(jnp.bfloat16)
    grad_q = inner_rows(normed, d_query)
    grad_k = inner_rows(normed, d_keys)
    grad_v = inner_rows(normed, d_values)
    grad_query, grad_key, grad_value = (
        lax.psum_scatter(
            grad_q[None].astype(jnp.bfloat16), "seg", scatter_dimension=1, tiled=True
        ).astype(jnp.float32),
        lax.psum_scatter(
            grad_k[None].astype(jnp.bfloat16), "seg", scatter_dimension=1, tiled=True
        ).astype(jnp.float32),
        lax.psum_scatter(
            grad_v[None].astype(jnp.bfloat16), "seg", scatter_dimension=1, tiled=True
        ).astype(jnp.float32),
    )
    grad_gain = lax.psum_scatter(grad_g[None], "seg", scatter_dimension=1, tiled=True)
    below, before = deliver(token_part, memory_part)
    return (below[None, None], before[None, None], grad_query, grad_key, grad_value, grad_gain)


SWAP = [(0, 1), (1, 0), (2, 3), (3, 2)]
ACROSS = [(1, 2), (2, 1)]
OUTWARD = [(1, 0), (2, 3)]
INWARD = [(0, 1), (3, 2)]
FAR_INWARD = [(0, 2), (3, 1)]
GRPS = [(0, 1), (1, 0)]


def full(shape_dtype=None):
    return pl.BlockSpec(memory_space=pltpu.VMEM)


def after(value, *others):
    return lax.optimization_barrier((value,) + others)[0]


def normalise_kernel(half, place_ref, tok_ref, mem_ref, gain_ref, n_ref, near_ref, far_ref):
    seg_len = tok_ref.shape[0]
    gain = gain_ref[...].astype(jnp.float32)

    def piece(rows):
        zf = rows.astype(jnp.float32)
        inv = lax.rsqrt(jnp.mean(zf * zf, -1, keepdims=True) + 1e-05)
        return (zf * inv * gain).astype(jnp.bfloat16)

    step = 32

    @pl.loop(0, seg_len // step)
    def _(i):
        at = pl.ds(pl.multiple_of(i * step, step), step)
        n_ref[at, :] = piece(tok_ref[at, :])

    n_ref[seg_len:, :] = piece(mem_ref[...])
    near = pl.multiple_of(place_ref[0], 128)
    far = pl.multiple_of(place_ref[1], 128)
    near_ref[...] = n_ref[:, pl.ds(near, half)]
    far_ref[...] = n_ref[:, pl.ds(far, half)]


def pieces_of(own, a, far, ya, yfar):
    quarter = a.shape[0]
    return (
        (own, 0, own.shape[0]),
        (a, 0, quarter),
        (far, 0, quarter),
        (far, quarter, quarter),
        (ya, 0, quarter),
        (yfar, 0, quarter),
        (yfar, quarter, quarter),
    )


def head_kernel(off_ref, n_ref, own, a, far, ya, yfar, hcot_ref, d_ref, qkv_ref):
    rows = n_ref.shape[0]
    total = None
    for i, (ref, start, count) in enumerate(pieces_of(own, a, far, ya, yfar)):
        at = pl.ds(pl.multiple_of(off_ref[i], 128), count)
        part = jnp.dot(
            n_ref[:, at], ref[start : start + count, :], preferred_element_type=jnp.float32
        )
        total = part if total is None else total + part
    qkv_ref[...] = total.astype(jnp.bfloat16)
    mem = rows - (rows // 128) * 128
    seg_len = rows - mem
    qw = GROUP * HD
    keys = jnp.concatenate([qkv_ref[:, qw : qw + HD], qkv_ref[seg_len:, qw : qw + HD]], 0)
    values = jnp.concatenate([qkv_ref[:, qw + HD :], qkv_ref[seg_len:, qw + HD :]], 0)
    scale = HD ** (-0.5)
    wide = rows + mem
    row = lax.broadcasted_iota(jnp.int32, (rows, wide), 0)
    col = lax.broadcasted_iota(jnp.int32, (rows, wide), 1)
    need = jnp.where(col < seg_len, col, jnp.where(col < rows, 0, col - mem))
    seen = row >= need
    d_keys = None
    d_values = None
    for g in range(GROUP):
        q = qkv_ref[:, g * HD : (g + 1) * HD]
        da = hcot_ref[:, g * HD : (g + 1) * HD]
        s = jnp.where(seen, times_t(q, keys) * scale, -1e30)
        e = jnp.exp(s - jnp.max(s, -1, keepdims=True))
        p = e / jnp.sum(e, -1, keepdims=True)
        dp = times_t(da, values)
        ds = (p * (dp - jnp.sum(p * dp, -1, keepdims=True)) * scale).astype(jnp.bfloat16)
        d_ref[:, g * HD : (g + 1) * HD] = jnp.dot(
            ds, keys, preferred_element_type=jnp.float32
        ).astype(jnp.bfloat16)
        dk = inner_rows(ds, q)
        dv = inner_rows(p.astype(jnp.bfloat16), da)
        d_keys = dk if d_keys is None else d_keys + dk
        d_values = dv if d_values is None else d_values + dv
    for at, both in ((qw, d_keys), (qw + HD, d_values)):
        d_ref[:seg_len, at : at + HD] = both[:seg_len].astype(jnp.bfloat16)
        d_ref[seg_len:, at : at + HD] = (both[seg_len:rows] + both[rows:]).astype(jnp.bfloat16)


def rows_kernel(off_ref, tok_ref, mem_ref, gain_ref, cot_ref, *refs):
    d_refs = refs[:HEADS]
    w_refs = refs[HEADS : 6 * HEADS]
    token_ref, memory_ref, gg_ref, dn_ref = refs[6 * HEADS :]
    seg_len = tok_ref.shape[0]
    all_pieces = [pieces_of(*w_refs[5 * c : 5 * c + 5]) for c in range(HEADS)]
    for i in range(len(all_pieces[0])):
        total = None
        for c in range(HEADS):
            ref, start, count = all_pieces[c][i]
            part = times_t(d_refs[c][...], ref[start : start + count, :])
            total = part if total is None else total + part
        dn_ref[:, pl.ds(pl.multiple_of(off_ref[i], 128), count)] = total
    gain = gain_ref[...].astype(jnp.float32)
    step = mem_ref.shape[0]

    def piece(rows, dn, cot):
        zf = rows.astype(jnp.float32)
        inv = lax.rsqrt(jnp.mean(zf * zf, -1, keepdims=True) + 1e-05)
        unit = zf * inv
        gg_ref[...] += jnp.sum(dn * unit, 0, keepdims=True)
        du = dn * gain
        out = cot.astype(jnp.float32) + inv * (
            du - unit * jnp.mean(du * unit, -1, keepdims=True)
        )
        return out.astype(jnp.bfloat16)

    gg_ref[...] = jnp.zeros_like(gg_ref)

    @pl.loop(0, seg_len // step)
    def _(i):
        at = pl.ds(pl.multiple_of(i * step, step), step)
        token_ref[at, :] = piece(tok_ref[at, :], dn_ref[at, :], cot_ref[at, :])

    memory_ref[...] = piece(mem_ref[...], dn_ref[seg_len:, :], cot_ref[seg_len:, :])


def grads_kernel(place_ref, nt_ref, d0, d1, d2, d3, other_ref, own_ref, dcat_ref):
    rows = d0.shape[0]
    for i, ref in enumerate((d0, d1, d2, d3)):
        dcat_ref[i * rows : (i + 1) * rows, :] = ref[...]
    block = own_ref.shape[0]
    other = pl.ds(pl.multiple_of(place_ref[2], 128), block)
    mine = pl.ds(pl.multiple_of(place_ref[3], 128), block)
    other_ref[...] = jnp.dot(
        nt_ref[other, :], dcat_ref[...], preferred_element_type=jnp.float32
    ).astype(jnp.bfloat16)
    own_ref[...] = jnp.dot(nt_ref[mine, :], dcat_ref[...], preferred_element_type=jnp.float32)


def on_line(inputs, memory, out_cot, head_cot, w_query, w_key, w_value, gain):
    tok = inputs[0, 0]
    mem = memory[0, 0]
    ocot = out_cot[0, 0]
    hcot = head_cot[0, 0]
    width = tok.shape[1]
    rows = tok.shape[0] + mem.shape[0]
    block = w_query.shape[1]
    quarter = block // 2
    qw = GROUP * HD
    cw = qw + 2 * HD
    z = lax.axis_index("seg")
    grp = lax.axis_index("grp")
    pair = z // 2
    inner = (z == 1) | (z == 2)
    partner = z + 1 - 2 * (z % 2)
    far_in = jnp.where(z < 2, 2, 1)
    far_out = jnp.where(z < 2, 3, 0)
    mine = grp * quarter
    theirs = (1 - grp) * quarter
    offsets = jnp.stack(
        [z * block]
        + [b * block + mine for b in (partner, far_out, far_in)]
        + [b * block + theirs for b in (partner, far_out, far_in)]
    ).astype(jnp.int32)
    places = jnp.stack(
        [pair * 2 * block, (1 - pair) * 2 * block, pair * block, (1 - pair) * block]
    ).astype(jnp.int32)

    smem = pl.BlockSpec(memory_space=pltpu.SMEM)
    vmem = pl.BlockSpec(memory_space=pltpu.VMEM)
    bf16 = jnp.bfloat16

    def shape(r, c, dtype=bf16):
        return jax.ShapeDtypeStruct((r, c), dtype)

    own = [
        jnp.concatenate(
            [
                w_query[0][:, c * qw : (c + 1) * qw],
                w_key[0][:, c * HD : (c + 1) * HD],
                w_value[0][:, c * HD : (c + 1) * HD],
            ],
            1,
        )
        for c in range(HEADS)
    ]
    half = [lax.dynamic_slice_in_dim(w, mine, quarter, 0) for w in own]

    normed, near, far = pl.pallas_call(
        functools.partial(normalise_kernel, 2 * block),
        out_shape=(shape(rows, width), shape(rows, 2 * block), shape(rows, 2 * block)),
        in_specs=[smem, vmem, vmem, vmem],
        out_specs=(vmem, vmem, vmem),
        compiler_params=pltpu.CompilerParams(vmem_limit_bytes=16 * MIB),
        cost_estimate=pl.CostEstimate(
            flops=8 * rows * width, bytes_accessed=6 * rows * width, transcendentals=rows
        ),
    )(places, tok, mem, gain)

    n_across = lax.ppermute(far, "seg", ACROSS)

    a, ya, b, c_, far_w, yfar = ([None] * HEADS for _ in range(6))
    for i in range(HEADS):
        send = half[i]
        if i == 3:
            send = after(send, b[0])
        a[i] = lax.ppermute(send, "seg", SWAP)
        ya[i] = lax.ppermute(a[i], "grp", GRPS)
        b[i] = lax.ppermute(jnp.concatenate([a[i], half[i]], 0), "seg", ACROSS)
        c_[i] = lax.ppermute(b[i], "seg", OUTWARD)
        far_w[i] = jnp.where(inner, b[i], c_[i])
        yfar[i] = lax.ppermute(far_w[i], "grp", GRPS)

    near_w = after(near, a[3])
    far_n = after(far, a[3])
    n_in = lax.ppermute(near_w, "seg", INWARD)
    n_far = lax.ppermute(far_n, "seg", FAR_INWARD)
    n_t = jnp.concatenate([near, n_in, n_across, n_far], 0).T

    pieces = [[own[i], a[i], far_w[i], ya[i], yfar[i]] for i in range(HEADS)]
    d = []
    recv = []
    kept = []
    for i in range(HEADS):
        d_i = pl.pallas_call(
            head_kernel,
            out_shape=shape(rows, cw),
            in_specs=[smem] + [vmem] * 7,
            out_specs=vmem,
            scratch_shapes=[pltpu.VMEM((rows, cw), bf16)],
            compiler_params=pltpu.CompilerParams(vmem_limit_bytes=32 * MIB),
            cost_estimate=pl.CostEstimate(
                flops=2 * rows * width * cw + 3 * 10 * GROUP * rows * rows * HD,
                bytes_accessed=2 * (width * cw + rows * width),
                transcendentals=GROUP * rows * rows,
            ),
        )(offsets, normed, *pieces[i], hcot[:, i * qw : (i + 1) * qw])
        d.append(d_i)
        d_across = lax.ppermute(d_i, "seg", ACROSS)
        d_in = lax.ppermute(d_i, "seg", INWARD)
        d_far = lax.ppermute(d_i, "seg", FAR_INWARD)
        other, mine_g = pl.pallas_call(
            grads_kernel,
            out_shape=(shape(block, cw), shape(block, cw, jnp.float32)),
            in_specs=[smem] + [vmem] * 5,
            out_specs=(vmem, vmem),
            scratch_shapes=[pltpu.VMEM((4 * rows, cw), bf16)],
            compiler_params=pltpu.CompilerParams(vmem_limit_bytes=32 * MIB),
            cost_estimate=pl.CostEstimate(
                flops=2 * 2 * block * 4 * rows * cw,
                bytes_accessed=2 * 4 * rows * (2 * block + cw) + 6 * block * cw,
                transcendentals=0,
            ),
        )(places, n_t, d_i, d_in, d_across, d_far)
        recv.append(lax.ppermute(other, "seg", OUTWARD))
        kept.append(mine_g)

    flat = [p for ps in pieces for p in ps]
    token_part, memory_part, grad_g = pl.pallas_call(
        rows_kernel,
        out_shape=(
            shape(tok.shape[0], width),
            shape(mem.shape[0], width),
            shape(1, width, jnp.float32),
        ),
        in_specs=[smem] + [vmem] * (4 + 6 * HEADS),
        out_specs=(vmem, vmem, vmem),
        scratch_shapes=[pltpu.VMEM((rows, width), jnp.float32)],
        compiler_params=pltpu.CompilerParams(vmem_limit_bytes=40 * MIB),
        cost_estimate=pl.CostEstimate(
            flops=2 * rows * width * cw * HEADS,
            bytes_accessed=2 * HEADS * cw * (width + rows) + 8 * rows * width,
            transcendentals=rows,
        ),
    )(offsets, tok, mem, gain, ocot, *d, *flat)

    below, before = deliver(token_part, memory_part)
    grad_gain = jnp.sum(
        lax.all_to_all(grad_g.reshape(4, width // 4), "seg", 0, 0, tiled=True), 0, keepdims=True
    )
    whole = [jnp.where(inner, k, r.astype(jnp.float32)) for k, r in zip(kept, recv)]
    grad_query = jnp.concatenate([w[:, :qw] for w in whole], 1)
    grad_key = jnp.concatenate([w[:, qw : qw + HD] for w in whole], 1)
    grad_value = jnp.concatenate([w[:, qw + HD :] for w in whole], 1)
    return (
        below[None, None],
        before[None, None],
        grad_query[None],
        grad_key[None],
        grad_value[None],
        grad_gain,
    )


def solution(mesh):
    in_specs = (
        P("section", ("grp", "seg"), None, None),
        P("section", ("grp", "seg"), None, None),
        P("section", ("grp", "seg"), None, None),
        P("section", ("grp", "seg"), None, None),
        P("section", "seg", None),
        P("section", "seg", None),
        P("section", "seg", None),
        P("section", None),
    )
    out_specs = (
        P("section", ("grp", "seg"), None, None),
        P("section", ("grp", "seg"), None, None),
        P(("grp", "section"), "seg", None),
        P(("grp", "section"), "seg", None),
        P(("grp", "section"), "seg", None),
        P(("grp", "section"), "seg"),
    )
    line = mesh.shape["seg"] == 4 and mesh.shape["grp"] == 2
    return jax.shard_map(
        on_line if line else on_device,
        mesh=mesh,
        in_specs=in_specs,
        out_specs=out_specs,
        check_vma=False,
    )
```

```python
import functools

import jax
import jax.numpy as jnp
from jax import lax
from jax.experimental import pallas as pl
from jax.experimental.pallas import tpu as pltpu
from jax.sharding import PartitionSpec as P

HEADS = 4
GROUP = 4
HD = 128
MIB = 1024 * 1024


def from_behind(block, axis, distance):
    devices = range(lax.axis_size(axis))
    route = [(i - distance, i) for i in devices if i - distance in devices]
    return lax.ppermute(block, axis, route)


def times_t(left, right):
    return lax.dot_general(
        left, right, (((1,), (1,)), ((), ())), preferred_element_type=jnp.float32
    )


def inner_rows(left, right):
    return lax.dot_general(
        left, right, (((0,), (0,)), ((), ())), preferred_element_type=jnp.float32
    )


def deliver(token_part, memory_part):
    below = from_behind(token_part, "section", -1)
    before = from_behind(memory_part, "seg", -1)
    return (below, before)


def on_device(inputs, memory, out_cot, head_cot, w_query, w_key, w_value, gain):
    whole_q, whole_k, whole_v = (
        lax.all_gather(w_query, "seg", axis=1, tiled=True),
        lax.all_gather(w_key, "seg", axis=1, tiled=True),
        lax.all_gather(w_value, "seg", axis=1, tiled=True),
    )
    wq = whole_q[0]
    wk = whole_k[0]
    wv = whole_v[0]
    tokens_in = inputs[0, 0]
    mem = memory[0, 0]
    ocot = out_cot[0, 0]
    hcot = head_cot[0, 0]
    gain_f = gain[0].astype(jnp.float32)
    mem_len = mem.shape[0]
    seg_len = tokens_in.shape[0]
    width = tokens_in.shape[1]
    query_width = wq.shape[1]
    rows = jnp.concatenate([mem, tokens_in, mem], 0)
    total = rows.shape[0]
    zf = rows.astype(jnp.float32)
    inv = lax.rsqrt(jnp.mean(zf * zf, -1, keepdims=True) + 1e-05)
    unit = zf * inv
    normed = (unit * gain_f).astype(jnp.bfloat16)
    query = (
        jnp.dot(normed, wq, preferred_element_type=jnp.float32)
        .astype(jnp.bfloat16)
        .reshape(total, HEADS, GROUP, HD)
    )
    keys = (
        jnp.dot(normed, wk, preferred_element_type=jnp.float32)
        .astype(jnp.bfloat16)
        .reshape(total, HEADS, HD)
    )
    values = (
        jnp.dot(normed, wv, preferred_element_type=jnp.float32)
        .astype(jnp.bfloat16)
        .reshape(total, HEADS, HD)
    )
    scale = HD ** (-0.5)
    scores = jnp.einsum("qhgd,khd->hgqk", query, keys, preferred_element_type=jnp.float32) * scale
    places = jnp.arange(total)
    causal = places[:, None] >= places[None, :]
    scores = jnp.where(causal[None, None], scores, -1e30)
    probs = jax.nn.softmax(scores, -1)
    probs_b = probs.astype(jnp.bfloat16)
    cot = jnp.concatenate([jnp.zeros((mem_len, width), jnp.bfloat16), ocot], 0)
    d_attn = jnp.concatenate([jnp.zeros((mem_len, query_width), jnp.bfloat16), hcot], 0)
    d_heads = d_attn.reshape(total, HEADS, GROUP, HD)
    d_probs = jnp.einsum("qhgd,khd->hgqk", d_heads, values, preferred_element_type=jnp.float32)
    d_scores = (probs * (d_probs - jnp.sum(probs * d_probs, -1, keepdims=True)) * scale).astype(
        jnp.bfloat16
    )
    d_values = jnp.einsum("hgqk,qhgd->khd", probs_b, d_heads, preferred_element_type=jnp.float32)
    d_values = d_values.astype(jnp.bfloat16).reshape(total, HEADS * HD)
    d_query = jnp.einsum("hgqk,khd->qhgd", d_scores, keys, preferred_element_type=jnp.float32)
    d_query = d_query.astype(jnp.bfloat16).reshape(total, query_width)
    d_keys = jnp.einsum("hgqk,qhgd->khd", d_scores, query, preferred_element_type=jnp.float32)
    d_keys = d_keys.astype(jnp.bfloat16).reshape(total, HEADS * HD)
    d_normed = times_t(d_query, wq) + times_t(d_keys, wk) + times_t(d_values, wv)
    grad_g = jnp.sum(d_normed * unit, 0)
    d_unit = d_normed * gain_f
    d_rows = cot.astype(jnp.float32) + inv * (
        d_unit - unit * jnp.mean(d_unit * unit, -1, keepdims=True)
    )
    token_part = d_rows[mem_len : mem_len + seg_len].astype(jnp.bfloat16)
    memory_part = (d_rows[:mem_len] + d_rows[mem_len + seg_len :]).astype(jnp.bfloat16)
    grad_q = inner_rows(normed, d_query)
    grad_k = inner_rows(normed, d_keys)
    grad_v = inner_rows(normed, d_values)
    grad_query, grad_key, grad_value = (
        lax.psum_scatter(
            grad_q[None].astype(jnp.bfloat16), "seg", scatter_dimension=1, tiled=True
        ).astype(jnp.float32),
        lax.psum_scatter(
            grad_k[None].astype(jnp.bfloat16), "seg", scatter_dimension=1, tiled=True
        ).astype(jnp.float32),
        lax.psum_scatter(
            grad_v[None].astype(jnp.bfloat16), "seg", scatter_dimension=1, tiled=True
        ).astype(jnp.float32),
    )
    grad_gain = lax.psum_scatter(grad_g[None], "seg", scatter_dimension=1, tiled=True)
    below, before = deliver(token_part, memory_part)
    return (below[None, None], before[None, None], grad_query, grad_key, grad_value, grad_gain)


SWAP = [(0, 1), (1, 0), (2, 3), (3, 2)]
ACROSS = [(1, 2), (2, 1)]
OUTWARD = [(1, 0), (2, 3)]
INWARD = [(0, 1), (3, 2)]
FAR_INWARD = [(0, 2), (3, 1)]
GRPS = [(0, 1), (1, 0)]


def normalise_kernel(half, place_ref, tok_ref, mem_ref, gain_ref, n_ref, near_ref, far_ref):
    seg_len = tok_ref.shape[0]
    gain = gain_ref[...].astype(jnp.float32)

    def piece(rows):
        zf = rows.astype(jnp.float32)
        inv = lax.rsqrt(jnp.mean(zf * zf, -1, keepdims=True) + 1e-05)
        return (zf * inv * gain).astype(jnp.bfloat16)

    step = 32

    @pl.loop(0, seg_len // step)
    def _(i):
        at = pl.ds(pl.multiple_of(i * step, step), step)
        n_ref[at, :] = piece(tok_ref[at, :])

    n_ref[seg_len:, :] = piece(mem_ref[...])
    near = pl.multiple_of(place_ref[0], 128)
    far = pl.multiple_of(place_ref[1], 128)
    near_ref[...] = n_ref[:, pl.ds(near, half)]
    far_ref[...] = n_ref[:, pl.ds(far, half)]


def halves_kernel(place_ref, wq, wk, wv, first, second, sems):
    quarter = first.shape[0] // 2
    qw = GROUP * HD
    at = pl.ds(pl.multiple_of(place_ref[4] * quarter, quarter), quarter)
    copies = []
    for c in range(HEADS):
        out = (first, second)[c // 2]
        to = slice((c % 2) * quarter, (c % 2 + 1) * quarter)
        for k, (w, start, wide) in enumerate(((wq, 0, qw), (wk, qw, HD), (wv, qw + HD, HD))):
            copies.append(
                pltpu.make_async_copy(
                    w.at[at, c * wide : (c + 1) * wide],
                    out.at[to, start : start + wide],
                    sems.at[3 * c + k],
                )
            )
    for copy in copies:
        copy.start()
    for copy in copies:
        copy.wait()


def fetch(copies):
    copies = [pltpu.make_async_copy(*c) for c in copies]
    for copy in copies:
        copy.start()
    return copies


def weight_copies(refs, starts, c, w_ref, sems):
    wq, wk, wv, a, far, ya, yfar = refs
    block = wq.shape[0]
    quarter = block // 2
    qw = GROUP * HD
    sources = [
        (wq.at[:, c * qw : (c + 1) * qw], slice(0, block), slice(0, qw)),
        (wk.at[:, c * HD : (c + 1) * HD], slice(0, block), slice(qw, qw + HD)),
        (wv.at[:, c * HD : (c + 1) * HD], slice(0, block), slice(qw + HD, qw + 2 * HD)),
    ]
    at = block
    for ref, start, rows in (
        (a, starts[0], quarter),
        (far, 0, 2 * quarter),
        (ya, starts[1], quarter),
        (yfar, 0, 2 * quarter),
    ):
        sources.append(
            (ref.at[start : start + rows, :], slice(at, at + rows), slice(0, w_ref.shape[1]))
        )
        at += rows
    return [(src, w_ref.at[r, k], sems.at[n]) for n, (src, r, k) in enumerate(sources)]


def piece_rows(block):
    quarter = block // 2
    sizes = [block] + [quarter] * 6
    waits = [(0, 1, 2), (3,), (4,), (), (5,), (6,), ()]
    at = 0
    for size, wait in zip(sizes, waits):
        yield at, size, wait
        at += size


def head_kernel(c, starts, off_ref, n_hbm, wq, wk, wv, a, far, ya, yfar, hcot_hbm, *refs):
    d_ref, dn_ref, w_ref, n_ref, h_ref, qkv_ref, sems = refs[-7:]
    rows = n_ref.shape[0]
    qw = GROUP * HD
    first = fetch([(n_hbm, n_ref, sems.at[7])])[0]
    copies = fetch(weight_copies((wq, wk, wv, a, far, ya, yfar), starts, c, w_ref, sems))
    cots = fetch([(hcot_hbm.at[:, c * qw : (c + 1) * qw], h_ref, sems.at[8])])[0]
    first.wait()
    total = None
    for i, (start, count, waits) in enumerate(piece_rows(wq.shape[0])):
        for k in waits:
            copies[k].wait()
        at = pl.ds(pl.multiple_of(off_ref[i], 128), count)
        part = jnp.dot(
            n_ref[:, at], w_ref[start : start + count, :], preferred_element_type=jnp.float32
        )
        total = part if total is None else total + part
    qkv_ref[...] = total.astype(jnp.bfloat16)
    cots.wait()
    mem = rows - (rows // 128) * 128
    seg_len = rows - mem
    keys = jnp.concatenate([qkv_ref[:, qw : qw + HD], qkv_ref[seg_len:, qw : qw + HD]], 0)
    values = jnp.concatenate([qkv_ref[:, qw + HD :], qkv_ref[seg_len:, qw + HD :]], 0)
    scale = HD ** (-0.5)
    wide = rows + mem
    row = lax.broadcasted_iota(jnp.int32, (rows, wide), 0)
    col = lax.broadcasted_iota(jnp.int32, (rows, wide), 1)
    need = jnp.where(col < seg_len, col, jnp.where(col < rows, 0, col - mem))
    seen = row >= need
    d_keys = None
    d_values = None
    for g in range(GROUP):
        q = qkv_ref[:, g * HD : (g + 1) * HD]
        da = h_ref[:, g * HD : (g + 1) * HD]
        s = jnp.where(seen, times_t(q, keys) * scale, -1e30)
        e = jnp.exp(s - jnp.max(s, -1, keepdims=True))
        p = e / jnp.sum(e, -1, keepdims=True)
        dp = times_t(da, values)
        ds = (p * (dp - jnp.sum(p * dp, -1, keepdims=True)) * scale).astype(jnp.bfloat16)
        d_ref[:, g * HD : (g + 1) * HD] = jnp.dot(
            ds, keys, preferred_element_type=jnp.float32
        ).astype(jnp.bfloat16)
        dk = inner_rows(ds, q)
        dv = inner_rows(p.astype(jnp.bfloat16), da)
        d_keys = dk if d_keys is None else d_keys + dk
        d_values = dv if d_values is None else d_values + dv
    for at, both in ((qw, d_keys), (qw + HD, d_values)):
        d_ref[:seg_len, at : at + HD] = both[:seg_len].astype(jnp.bfloat16)
        d_ref[seg_len:, at : at + HD] = (both[seg_len:rows] + both[rows:]).astype(jnp.bfloat16)
    for i, (start, count, _) in enumerate(piece_rows(wq.shape[0])):
        at = pl.ds(pl.multiple_of(off_ref[i], 128), count)
        part = times_t(d_ref[...], w_ref[start : start + count, :])
        dn_ref[:, at] = refs[0][:, at] + part if len(refs) > 7 else part


def rows_kernel(dn_ref, tok_ref, mem_ref, gain_ref, cot_ref, token_ref, memory_ref, gg_ref):
    seg_len = tok_ref.shape[0]
    gain = gain_ref[...].astype(jnp.float32)
    step = mem_ref.shape[0]

    def piece(rows, dn, cot):
        zf = rows.astype(jnp.float32)
        inv = lax.rsqrt(jnp.mean(zf * zf, -1, keepdims=True) + 1e-05)
        unit = zf * inv
        gg_ref[...] += jnp.sum(dn * unit, 0, keepdims=True)
        du = dn * gain
        out = cot.astype(jnp.float32) + inv * (
            du - unit * jnp.mean(du * unit, -1, keepdims=True)
        )
        return out.astype(jnp.bfloat16)

    gg_ref[...] = jnp.zeros_like(gg_ref)

    @pl.loop(0, seg_len // step)
    def _(i):
        at = pl.ds(pl.multiple_of(i * step, step), step)
        token_ref[at, :] = piece(tok_ref[at, :], dn_ref[at, :], cot_ref[at, :])

    memory_ref[...] = piece(mem_ref[...], dn_ref[seg_len:, :], cot_ref[seg_len:, :])


def turn_kernel(n0, n1, n2, n3, out_ref, cat_ref):
    rows = n0.shape[0]
    for i, ref in enumerate((n0, n1, n2, n3)):
        cat_ref[i * rows : (i + 1) * rows, :] = ref[...]
    for i in range(out_ref.shape[0] // 256):
        at = slice(256 * i, 256 * (i + 1))
        out_ref[at, :] = cat_ref[:, at].T


def grads_kernel(place_ref, nt_ref, d0, d1, d2, d3, *refs):
    other_ref, q_ref, k_ref, v_ref, dcat_ref = refs[-5:]

    @pl.when(place_ref[5] == 1)
    def _():
        rows = d0.shape[0]
        for i, ref in enumerate((d0, d1, d2, d3)):
            dcat_ref[i * rows : (i + 1) * rows, :] = ref[...]
        block = other_ref.shape[0]
        qw = GROUP * HD
        other = pl.ds(pl.multiple_of(place_ref[2], 128), block)
        mine = pl.ds(pl.multiple_of(place_ref[3], 128), block)
        other_ref[...] = jnp.dot(
            nt_ref[other, :], dcat_ref[...], preferred_element_type=jnp.float32
        ).astype(jnp.bfloat16)
        total = jnp.dot(nt_ref[mine, :], dcat_ref[...], preferred_element_type=jnp.float32)
        q_ref[...] = total[:, :qw]
        k_ref[...] = total[:, qw : qw + HD]
        v_ref[...] = total[:, qw + HD :]


def place_kernel(heads, place_ref, *refs):
    recvs = refs[: len(heads)]
    q_ref, k_ref, v_ref, q_buf, k_buf, v_buf, sems = refs[-7:]
    qw = GROUP * HD

    @pl.when(place_ref[5] == 0)
    def _():
        for c, recv in zip(heads, recvs):
            q_buf[...] = recv[:, :qw].astype(jnp.float32)
            k_buf[...] = recv[:, qw : qw + HD].astype(jnp.float32)
            v_buf[...] = recv[:, qw + HD :].astype(jnp.float32)
            copies = [
                pltpu.make_async_copy(buf, ref.at[:, c * wide : (c + 1) * wide], sems.at[k])
                for k, (buf, ref, wide) in enumerate(
                    ((q_buf, q_ref, qw), (k_buf, k_ref, HD), (v_buf, v_ref, HD))
                )
            ]
            for copy in copies:
                copy.start()
            for copy in copies:
                copy.wait()


def copy_kernel(*refs):
    count = len(refs) // 2
    for src, dst in zip(refs[:count], refs[count:]):
        dst[...] = src[...]


class Order:
    def __init__(self, mark):
        self.mark = mark

    def point(self, *values):
        out = lax.optimization_barrier((self.mark,) + values)
        self.mark = out[0]
        return out[1] if len(values) == 1 else out[1:]


def on_line(inputs, memory, out_cot, head_cot, w_query, w_key, w_value, gain):
    tok = inputs[0, 0]
    mem = memory[0, 0]
    ocot = out_cot[0, 0]
    hcot = head_cot[0, 0]
    ws = (w_query[0], w_key[0], w_value[0])
    width = tok.shape[1]
    rows = tok.shape[0] + mem.shape[0]
    block = w_query.shape[1]
    quarter = block // 2
    qw = GROUP * HD
    cw = qw + 2 * HD
    z = lax.axis_index("seg")
    grp = lax.axis_index("grp")
    pair = z // 2
    inner = (z == 1) | (z == 2)
    partner = z + 1 - 2 * (z % 2)
    far_in = jnp.where(z < 2, 2, 1)
    far_out = jnp.where(z < 2, 3, 0)
    mine = grp * quarter
    theirs = (1 - grp) * quarter
    offsets = jnp.stack(
        [z * block]
        + [b * block + mine for b in (partner, far_out, far_in)]
        + [b * block + theirs for b in (partner, far_out, far_in)]
    ).astype(jnp.int32)
    places = jnp.stack(
        [
            pair * 2 * block,
            (1 - pair) * 2 * block,
            pair * block,
            (1 - pair) * block,
            grp,
            inner.astype(jnp.int32),
        ]
    ).astype(jnp.int32)

    smem = pl.BlockSpec(memory_space=pltpu.SMEM)
    vmem = pl.BlockSpec(memory_space=pltpu.VMEM)
    bf16 = jnp.bfloat16
    f32 = jnp.float32

    def shape(r, c, dtype=bf16):
        return jax.ShapeDtypeStruct((r, c), dtype)

    free = pl.CostEstimate(flops=0, bytes_accessed=0, transcendentals=0)
    anywhere = pl.BlockSpec(memory_space=pl.ANY)
    hbm = pl.BlockSpec(memory_space=pltpu.HBM)

    def part(r, c, at=0):
        return pl.BlockSpec((r, c), lambda *_: (0, at), pipeline_mode=pl.Buffered(1))

    def own_w(c):
        return [part(block, qw, c), part(block, HD, c), part(block, HD, c)]

    def call(kernel, outs, args, specs=None, mib=20, scratch=(), smems=1, aliases=None, out_specs=None):
        specs = specs or {}
        out_specs = out_specs or {}
        args = tuple(
            pltpu.with_memory_space_constraint(x, pltpu.HBM) if specs.get(k) is hbm else x
            for k, x in enumerate(args)
        )
        many = isinstance(outs, tuple)
        out_list = outs if many else (outs,)
        ins = [smem] * smems + [specs.get(k) or part(*args[k].shape) for k in range(smems, len(args))]
        ends = tuple(out_specs.get(k) or part(*o.shape) for k, o in enumerate(out_list))
        return pl.pallas_call(
            kernel,
            grid=(1,),
            out_shape=outs,
            in_specs=ins,
            out_specs=ends if many else ends[0],
            scratch_shapes=scratch,
            input_output_aliases=aliases or {},
            compiler_params=pltpu.CompilerParams(vmem_limit_bytes=mib * MIB),
            cost_estimate=free,
        )(*args)

    def permute(value, axis, route):
        return lax.ppermute(value, axis, route)

    def z_and(value):
        return jnp.concatenate(value, 0)

    order = Order(z.astype(jnp.int32))
    h01, h23 = call(
        halves_kernel,
        (shape(block, cw), shape(block, cw)),
        (places,) + ws,
        specs={k: hbm for k in (1, 2, 3)},
        scratch=[pltpu.SemaphoreType.DMA((12,))],
    )

    def head(i, pieces, starts, dn=()):
        args = (offsets, normed) + ws + tuple(pieces) + (hcot,)
        n = len(args)
        return call(
            functools.partial(head_kernel, i, starts),
            (shape(rows, cw), shape(rows, width, f32)),
            args + dn,
            specs={k: hbm for k in range(1, n)} | {6: anywhere},
            scratch=[
                pltpu.VMEM((width, cw), bf16),
                pltpu.VMEM((rows, width), bf16),
                pltpu.VMEM((rows, qw), bf16),
                pltpu.VMEM((rows, cw), bf16),
                pltpu.SemaphoreType.DMA((9,)),
            ],
            aliases={n: 1} if dn else None,
        )

    whole_shapes = tuple(shape(block, n * HEADS, f32) for n in (qw, HD, HD))

    def grads(i, n_t, ds, before):
        args = (places, n_t) + tuple(ds) + tuple(before)
        out = call(
            grads_kernel,
            (shape(block, cw),) + whole_shapes,
            args,
            specs={6 + k: anywhere for k in range(len(before))},
            out_specs={1 + k: spec for k, spec in enumerate(own_w(i))},
            scratch=[pltpu.VMEM((4 * rows, cw), bf16)],
            aliases={6 + k: 1 + k for k in range(len(before))},
        )
        return out[0], out[1:]

    def place(heads, recvs, before):
        n = 1 + len(heads)
        return call(
            functools.partial(place_kernel, heads),
            whole_shapes,
            (places,) + tuple(recvs) + tuple(before),
            specs={n + k: anywhere for k in range(3)},
            out_specs={k: anywhere for k in range(3)},
            scratch=[pltpu.VMEM((block, n), f32) for n in (qw, HD, HD)]
            + [pltpu.SemaphoreType.DMA((3,))],
            aliases={n + k: k for k in range(3)},
        )

    def pick(b, c):
        return jnp.where(inner, b, c)

    def send(d):
        return [permute(d, "seg", r) for r in (FAR_INWARD, ACROSS, INWARD)]

    a01 = permute(h01, "seg", SWAP)
    normed, near, far = call(
        functools.partial(normalise_kernel, 2 * block),
        (shape(rows, width), shape(rows, 2 * block), shape(rows, 2 * block)),
        (places, tok, mem, gain),
    )
    n_across = permute(far, "seg", ACROSS)
    a01, n_across, h01, h23, normed, near, far = order.point(
        a01, n_across, h01, h23, normed, near, far
    )
    a23 = permute(h23, "seg", SWAP)
    b0 = permute(z_and([a01[:quarter], h01[:quarter]]), "seg", ACROSS)
    ya01 = permute(a01, "grp", GRPS)
    to1 = z_and([a01[quarter:], h01[quarter:]])
    b0, ya01, a23, to1, h23, near, far = order.point(b0, ya01, a23, to1, h23, near, far)
    ya23 = permute(a23, "grp", GRPS)
    n_in = permute(near, "seg", INWARD)
    b1 = permute(to1, "seg", ACROSS)
    c0 = permute(b0, "seg", OUTWARD)
    to2 = z_and([a23[:quarter], h23[:quarter]])
    to3 = z_and([a23[quarter:], h23[quarter:]])
    f0 = pick(b0, c0)
    ya23, n_in, b1, f0, to2, to3, far = order.point(ya23, n_in, b1, f0, to2, to3, far)
    yf0 = permute(f0, "grp", GRPS)
    n_far = permute(far, "seg", FAR_INWARD)
    b2 = permute(to2, "seg", ACROSS)
    c1 = permute(b1, "seg", OUTWARD)
    f1 = pick(b1, c1)
    yf0, n_far, b2, f1, to3 = order.point(yf0, n_far, b2, f1, to3)
    yf1 = permute(f1, "grp", GRPS)
    b3 = permute(to3, "seg", ACROSS)
    c2 = permute(b2, "seg", OUTWARD)
    d0, dn = head(0, (a01, f0, ya01, yf0), (0, 0))
    f2 = pick(b2, c2)
    yf1, b3, f2, d0, dn = order.point(yf1, b3, f2, d0, dn)
    yf2 = permute(f2, "grp", GRPS)
    c3 = permute(b3, "seg", OUTWARD)
    x0 = send(d0)
    d1, dn = head(1, (a01, f1, ya01, yf1), (quarter, quarter), (dn,))
    n_t = call(
        turn_kernel,
        shape(2 * block, 4 * rows),
        (near, n_in, n_across, n_far),
        scratch=[pltpu.VMEM((4 * rows, 2 * block), bf16)],
        smems=0,
    )
    f3 = pick(b3, c3)
    yf2, f3, x00, x01, x02, d1, dn, n_t = order.point(yf2, f3, *x0, d1, dn, n_t)
    yf3 = permute(f3, "grp", GRPS)
    x1 = send(d1)
    o0, whole = grads(0, n_t, (d0, x02, x01, x00), ())
    r0 = permute(o0, "seg", OUTWARD)
    d2, dn = head(2, (a23, f2, ya23, yf2), (0, 0), (dn,))
    yf3, x10, x11, x12, d2, dn, o0 = order.point(yf3, *x1, d2, dn, o0)
    x2 = send(d2)
    o1, whole = grads(1, n_t, (d1, x12, x11, x10), whole)
    r1 = permute(o1, "seg", OUTWARD)
    d3, dn = head(3, (a23, f3, ya23, yf3), (quarter, quarter), (dn,))
    x20, x21, x22, d3, r0, dn, o1 = order.point(*x2, d3, r0, dn, o1)
    x3 = send(d3)
    o2, whole = grads(2, n_t, (d2, x22, x21, x20), whole)
    r2 = permute(o2, "seg", OUTWARD)
    token_part, memory_part, grad_g = call(
        rows_kernel,
        (shape(tok.shape[0], width), shape(mem.shape[0], width), shape(1, width, f32)),
        (dn, tok, mem, gain, ocot),
        smems=0,
    )
    x30, x31, x32, r1, r2, token_part, memory_part, grad_g = order.point(
        *x3, r1, r2, token_part, memory_part, grad_g
    )
    o3, whole = grads(3, n_t, (d3, x32, x31, x30), whole)
    r3 = permute(o3, "seg", OUTWARD)
    below, before = deliver(token_part, memory_part)
    gains = lax.all_to_all(grad_g.reshape(4, width // 4), "seg", 0, 0, tiled=True)
    grad_gain = jnp.sum(gains, 0, keepdims=True)
    whole = place((0, 1, 2), (r0, r1, r2), whole)
    below = call(copy_kernel, shape(tok.shape[0], width), (below,), smems=0)
    r3, below, q_, k_, v_ = order.point(r3, below, *whole)
    grad_query, grad_key, grad_value = place((3,), (r3,), (q_, k_, v_))
    return (
        below[None, None],
        before[None, None],
        grad_query[None],
        grad_key[None],
        grad_value[None],
        grad_gain,
    )


def solution(mesh):
    in_specs = (
        P("section", ("grp", "seg"), None, None),
        P("section", ("grp", "seg"), None, None),
        P("section", ("grp", "seg"), None, None),
        P("section", ("grp", "seg"), None, None),
        P("section", "seg", None),
        P("section", "seg", None),
        P("section", "seg", None),
        P("section", None),
    )
    out_specs = (
        P("section", ("grp", "seg"), None, None),
        P("section", ("grp", "seg"), None, None),
        P(("grp", "section"), "seg", None),
        P(("grp", "section"), "seg", None),
        P(("grp", "section"), "seg", None),
        P(("grp", "section"), "seg"),
    )
    line = mesh.shape["seg"] == 4 and mesh.shape["grp"] == 2
    return jax.shard_map(
        on_line if line else on_device,
        mesh=mesh,
        in_specs=in_specs,
        out_specs=out_specs,
        check_vma=False,
    )
```

```python
import functools

import jax
import jax.numpy as jnp
from jax import lax
from jax.experimental import pallas as pl
from jax.experimental.pallas import tpu as pltpu
from jax.sharding import PartitionSpec as P

HEADS = 4
GROUP = 4
HD = 128
MIB = 1024 * 1024


def from_behind(block, axis, distance):
    devices = range(lax.axis_size(axis))
    route = [(i - distance, i) for i in devices if i - distance in devices]
    return lax.ppermute(block, axis, route)


def times_t(left, right):
    return lax.dot_general(
        left, right, (((1,), (1,)), ((), ())), preferred_element_type=jnp.float32
    )


def inner_rows(left, right):
    return lax.dot_general(
        left, right, (((0,), (0,)), ((), ())), preferred_element_type=jnp.float32
    )


def deliver(token_part, memory_part):
    below = from_behind(token_part, "section", -1)
    before = from_behind(memory_part, "seg", -1)
    return (below, before)


def on_device(inputs, memory, out_cot, head_cot, w_query, w_key, w_value, gain):
    whole_q, whole_k, whole_v = (
        lax.all_gather(w_query, "seg", axis=1, tiled=True),
        lax.all_gather(w_key, "seg", axis=1, tiled=True),
        lax.all_gather(w_value, "seg", axis=1, tiled=True),
    )
    wq = whole_q[0]
    wk = whole_k[0]
    wv = whole_v[0]
    tokens_in = inputs[0, 0]
    mem = memory[0, 0]
    ocot = out_cot[0, 0]
    hcot = head_cot[0, 0]
    gain_f = gain[0].astype(jnp.float32)
    mem_len = mem.shape[0]
    seg_len = tokens_in.shape[0]
    width = tokens_in.shape[1]
    query_width = wq.shape[1]
    rows = jnp.concatenate([mem, tokens_in, mem], 0)
    total = rows.shape[0]
    zf = rows.astype(jnp.float32)
    inv = lax.rsqrt(jnp.mean(zf * zf, -1, keepdims=True) + 1e-05)
    unit = zf * inv
    normed = (unit * gain_f).astype(jnp.bfloat16)
    query = (
        jnp.dot(normed, wq, preferred_element_type=jnp.float32)
        .astype(jnp.bfloat16)
        .reshape(total, HEADS, GROUP, HD)
    )
    keys = (
        jnp.dot(normed, wk, preferred_element_type=jnp.float32)
        .astype(jnp.bfloat16)
        .reshape(total, HEADS, HD)
    )
    values = (
        jnp.dot(normed, wv, preferred_element_type=jnp.float32)
        .astype(jnp.bfloat16)
        .reshape(total, HEADS, HD)
    )
    scale = HD ** (-0.5)
    scores = jnp.einsum("qhgd,khd->hgqk", query, keys, preferred_element_type=jnp.float32) * scale
    places = jnp.arange(total)
    causal = places[:, None] >= places[None, :]
    scores = jnp.where(causal[None, None], scores, -1e30)
    probs = jax.nn.softmax(scores, -1)
    probs_b = probs.astype(jnp.bfloat16)
    cot = jnp.concatenate([jnp.zeros((mem_len, width), jnp.bfloat16), ocot], 0)
    d_attn = jnp.concatenate([jnp.zeros((mem_len, query_width), jnp.bfloat16), hcot], 0)
    d_heads = d_attn.reshape(total, HEADS, GROUP, HD)
    d_probs = jnp.einsum("qhgd,khd->hgqk", d_heads, values, preferred_element_type=jnp.float32)
    d_scores = (probs * (d_probs - jnp.sum(probs * d_probs, -1, keepdims=True)) * scale).astype(
        jnp.bfloat16
    )
    d_values = jnp.einsum("hgqk,qhgd->khd", probs_b, d_heads, preferred_element_type=jnp.float32)
    d_values = d_values.astype(jnp.bfloat16).reshape(total, HEADS * HD)
    d_query = jnp.einsum("hgqk,khd->qhgd", d_scores, keys, preferred_element_type=jnp.float32)
    d_query = d_query.astype(jnp.bfloat16).reshape(total, query_width)
    d_keys = jnp.einsum("hgqk,qhgd->khd", d_scores, query, preferred_element_type=jnp.float32)
    d_keys = d_keys.astype(jnp.bfloat16).reshape(total, HEADS * HD)
    d_normed = times_t(d_query, wq) + times_t(d_keys, wk) + times_t(d_values, wv)
    grad_g = jnp.sum(d_normed * unit, 0)
    d_unit = d_normed * gain_f
    d_rows = cot.astype(jnp.float32) + inv * (
        d_unit - unit * jnp.mean(d_unit * unit, -1, keepdims=True)
    )
    token_part = d_rows[mem_len : mem_len + seg_len].astype(jnp.bfloat16)
    memory_part = (d_rows[:mem_len] + d_rows[mem_len + seg_len :]).astype(jnp.bfloat16)
    grad_q = inner_rows(normed, d_query)
    grad_k = inner_rows(normed, d_keys)
    grad_v = inner_rows(normed, d_values)
    grad_query, grad_key, grad_value = (
        lax.psum_scatter(
            grad_q[None].astype(jnp.bfloat16), "seg", scatter_dimension=1, tiled=True
        ).astype(jnp.float32),
        lax.psum_scatter(
            grad_k[None].astype(jnp.bfloat16), "seg", scatter_dimension=1, tiled=True
        ).astype(jnp.float32),
        lax.psum_scatter(
            grad_v[None].astype(jnp.bfloat16), "seg", scatter_dimension=1, tiled=True
        ).astype(jnp.float32),
    )
    grad_gain = lax.psum_scatter(grad_g[None], "seg", scatter_dimension=1, tiled=True)
    below, before = deliver(token_part, memory_part)
    return (below[None, None], before[None, None], grad_query, grad_key, grad_value, grad_gain)


SWAP = [(0, 1), (1, 0), (2, 3), (3, 2)]
ACROSS = [(1, 2), (2, 1)]
OUTWARD = [(1, 0), (2, 3)]
INWARD = [(0, 1), (3, 2)]
FAR_INWARD = [(0, 2), (3, 1)]
GRPS = [(0, 1), (1, 0)]


def normalise_kernel(half, place_ref, tok_ref, mem_ref, gain_ref, n_ref, near_ref, far_ref):
    seg_len = tok_ref.shape[0]
    gain = gain_ref[...].astype(jnp.float32)

    def piece(rows):
        zf = rows.astype(jnp.float32)
        inv = lax.rsqrt(jnp.mean(zf * zf, -1, keepdims=True) + 1e-05)
        return (zf * inv * gain).astype(jnp.bfloat16)

    step = 32

    @pl.loop(0, seg_len // step)
    def _(i):
        at = pl.ds(pl.multiple_of(i * step, step), step)
        n_ref[at, :] = piece(tok_ref[at, :])

    n_ref[seg_len:, :] = piece(mem_ref[...])
    near = pl.multiple_of(place_ref[0], 128)
    far = pl.multiple_of(place_ref[1], 128)
    near_ref[...] = n_ref[:, pl.ds(near, half)]
    far_ref[...] = n_ref[:, pl.ds(far, half)]


def halves_kernel(place_ref, wq, wk, wv, first, second, sems):
    quarter = first.shape[0] // 2
    qw = GROUP * HD
    at = pl.ds(pl.multiple_of(place_ref[4] * quarter, quarter), quarter)
    copies = []
    for c in range(HEADS):
        out = (first, second)[c // 2]
        to = slice((c % 2) * quarter, (c % 2 + 1) * quarter)
        for k, (w, start, wide) in enumerate(((wq, 0, qw), (wk, qw, HD), (wv, qw + HD, HD))):
            copies.append(
                pltpu.make_async_copy(
                    w.at[at, c * wide : (c + 1) * wide],
                    out.at[to, start : start + wide],
                    sems.at[3 * c + k],
                )
            )
    for copy in copies:
        copy.start()
    for copy in copies:
        copy.wait()


def fetch(copies):
    copies = [pltpu.make_async_copy(*c) for c in copies]
    for copy in copies:
        copy.start()
    return copies


def weight_copies(refs, starts, c, w_ref, sems):
    wq, wk, wv, a, far, ya, yfar = refs
    block = wq.shape[0]
    quarter = block // 2
    qw = GROUP * HD
    sources = [
        (wq.at[:, c * qw : (c + 1) * qw], slice(0, block), slice(0, qw)),
        (wk.at[:, c * HD : (c + 1) * HD], slice(0, block), slice(qw, qw + HD)),
        (wv.at[:, c * HD : (c + 1) * HD], slice(0, block), slice(qw + HD, qw + 2 * HD)),
    ]
    at = block
    for ref, start, rows in (
        (a, starts[0], quarter),
        (far, 0, 2 * quarter),
        (ya, starts[1], quarter),
        (yfar, 0, 2 * quarter),
    ):
        sources.append(
            (ref.at[start : start + rows, :], slice(at, at + rows), slice(0, w_ref.shape[1]))
        )
        at += rows
    return [(src, w_ref.at[r, k], sems.at[n]) for n, (src, r, k) in enumerate(sources)]


def piece_rows(block):
    quarter = block // 2
    sizes = [block] + [quarter] * 6
    waits = [(0, 1, 2), (3,), (4,), (), (5,), (6,), ()]
    at = 0
    for size, wait in zip(sizes, waits):
        yield at, size, wait
        at += size


def head_kernel(c, starts, off_ref, n_hbm, wq, wk, wv, a, far, ya, yfar, hcot_hbm, *refs):
    d_ref, dn_ref, w_ref, n_ref, h_ref, qkv_ref, sems = refs[-7:]
    rows = n_ref.shape[0]
    qw = GROUP * HD
    first = fetch([(n_hbm, n_ref, sems.at[7])])[0]
    copies = fetch(weight_copies((wq, wk, wv, a, far, ya, yfar), starts, c, w_ref, sems))
    cots = fetch([(hcot_hbm.at[:, c * qw : (c + 1) * qw], h_ref, sems.at[8])])[0]
    first.wait()
    total = None
    for i, (start, count, waits) in enumerate(piece_rows(wq.shape[0])):
        for k in waits:
            copies[k].wait()
        at = pl.ds(pl.multiple_of(off_ref[i], 128), count)
        part = jnp.dot(
            n_ref[:, at], w_ref[start : start + count, :], preferred_element_type=jnp.float32
        )
        total = part if total is None else total + part
    qkv_ref[...] = total.astype(jnp.bfloat16)
    cots.wait()
    mem = rows - (rows // 128) * 128
    seg_len = rows - mem
    keys = jnp.concatenate([qkv_ref[:, qw : qw + HD], qkv_ref[seg_len:, qw : qw + HD]], 0)
    values = jnp.concatenate([qkv_ref[:, qw + HD :], qkv_ref[seg_len:, qw + HD :]], 0)
    scale = HD ** (-0.5)
    wide = rows + mem
    row = lax.broadcasted_iota(jnp.int32, (rows, wide), 0)
    col = lax.broadcasted_iota(jnp.int32, (rows, wide), 1)
    need = jnp.where(col < seg_len, col, jnp.where(col < rows, 0, col - mem))
    seen = row >= need
    d_keys = None
    d_values = None
    for g in range(GROUP):
        q = qkv_ref[:, g * HD : (g + 1) * HD]
        da = h_ref[:, g * HD : (g + 1) * HD]
        s = jnp.where(seen, times_t(q, keys) * scale, -1e30)
        e = jnp.exp(s - jnp.max(s, -1, keepdims=True))
        p = e / jnp.sum(e, -1, keepdims=True)
        dp = times_t(da, values)
        ds = (p * (dp - jnp.sum(p * dp, -1, keepdims=True)) * scale).astype(jnp.bfloat16)
        d_ref[:, g * HD : (g + 1) * HD] = jnp.dot(
            ds, keys, preferred_element_type=jnp.float32
        ).astype(jnp.bfloat16)
        dk = inner_rows(ds, q)
        dv = inner_rows(p.astype(jnp.bfloat16), da)
        d_keys = dk if d_keys is None else d_keys + dk
        d_values = dv if d_values is None else d_values + dv
    for at, both in ((qw, d_keys), (qw + HD, d_values)):
        d_ref[:seg_len, at : at + HD] = both[:seg_len].astype(jnp.bfloat16)
        d_ref[seg_len:, at : at + HD] = (both[seg_len:rows] + both[rows:]).astype(jnp.bfloat16)
    for i, (start, count, _) in enumerate(piece_rows(wq.shape[0])):
        at = pl.ds(pl.multiple_of(off_ref[i], 128), count)
        part = times_t(d_ref[...], w_ref[start : start + count, :])
        dn_ref[:, at] = refs[0][:, at] + part if len(refs) > 7 else part


def rows_kernel(dn_ref, tok_ref, mem_ref, gain_ref, cot_ref, token0, token1, memory_ref, gg_ref):
    seg_len = tok_ref.shape[0]
    gain = gain_ref[...].astype(jnp.float32)
    step = mem_ref.shape[0]

    def piece(rows, dn, cot):
        zf = rows.astype(jnp.float32)
        inv = lax.rsqrt(jnp.mean(zf * zf, -1, keepdims=True) + 1e-05)
        unit = zf * inv
        gg_ref[...] += jnp.sum(dn * unit, 0, keepdims=True)
        du = dn * gain
        out = cot.astype(jnp.float32) + inv * (
            du - unit * jnp.mean(du * unit, -1, keepdims=True)
        )
        return out.astype(jnp.bfloat16)

    gg_ref[...] = jnp.zeros_like(gg_ref)

    for k, token_ref in enumerate((token0, token1)):

        @pl.loop(0, seg_len // 2 // step)
        def _(i, token_ref=token_ref, k=k):
            to = pl.ds(pl.multiple_of(i * step, step), step)
            at = pl.ds(pl.multiple_of(k * seg_len // 2 + i * step, step), step)
            token_ref[to, :] = piece(tok_ref[at, :], dn_ref[at, :], cot_ref[at, :])

    memory_ref[...] = piece(mem_ref[...], dn_ref[seg_len:, :], cot_ref[seg_len:, :])


def turn_kernel(n0, n1, n2, n3, out_ref, cat_ref):
    rows = n0.shape[0]
    for i, ref in enumerate((n0, n1, n2, n3)):
        cat_ref[i * rows : (i + 1) * rows, :] = ref[...]
    for i in range(out_ref.shape[0] // 256):
        at = slice(256 * i, 256 * (i + 1))
        out_ref[at, :] = cat_ref[:, at].T


def grads_kernel(first, count, own, place_ref, nt_ref, d0, d1, d2, d3, *refs):
    dcat_ref = refs[-1]
    outs = refs[-4 - (count > 0) : -1] if own else refs[-2:-1]

    @pl.when(place_ref[5] == 1)
    def _():
        rows = d0.shape[0]
        for i, ref in enumerate((d0, d1, d2, d3)):
            dcat_ref[i * rows : (i + 1) * rows, :] = ref[...]
        block = nt_ref.shape[0] // 2
        qw = GROUP * HD
        if count:
            other = pl.ds(pl.multiple_of(place_ref[2] + first, 128), count)
            outs[0][...] = jnp.dot(
                nt_ref[other, :], dcat_ref[...], preferred_element_type=jnp.float32
            ).astype(jnp.bfloat16)
        if own:
            mine = pl.ds(pl.multiple_of(place_ref[3], 128), block)
            q_ref, k_ref, v_ref = outs[-3:]
            total = jnp.dot(nt_ref[mine, :], dcat_ref[...], preferred_element_type=jnp.float32)
            q_ref[...] = total[:, :qw]
            k_ref[...] = total[:, qw : qw + HD]
            v_ref[...] = total[:, qw + HD :]


def place_kernel(spots, place_ref, *refs):
    recvs = refs[: len(spots)]
    q_ref, k_ref, v_ref, q_buf, k_buf, v_buf, sems = refs[-7:]
    qw = GROUP * HD

    @pl.when(place_ref[5] == 0)
    def _():
        waiting = []
        for n, ((c, first), recv) in enumerate(zip(spots, recvs)):
            count = recv.shape[0]
            for k, (buf, ref, at, wide) in enumerate(
                ((q_buf, q_ref, 0, qw), (k_buf, k_ref, qw, HD), (v_buf, v_ref, qw + HD, HD))
            ):
                buf[n, :count, :] = recv[:, at : at + wide].astype(jnp.float32)
                copy = pltpu.make_async_copy(
                    buf.at[n, :count, :],
                    ref.at[first : first + count, c * wide : (c + 1) * wide],
                    sems.at[n, k],
                )
                copy.start()
                waiting.append(copy)
        for copy in waiting:
            copy.wait()


def copy_kernel(*refs):
    out_ref = refs[-1]
    at = 0
    for ref in refs[:-1]:
        out_ref[at : at + ref.shape[0], :] = ref[...]
        at += ref.shape[0]


class Order:
    def __init__(self, mark):
        self.mark = mark

    def point(self, *values):
        out = lax.optimization_barrier((self.mark,) + values)
        self.mark = out[0]
        return out[1] if len(values) == 1 else out[1:]


def on_line(inputs, memory, out_cot, head_cot, w_query, w_key, w_value, gain):
    tok = inputs[0, 0]
    mem = memory[0, 0]
    ocot = out_cot[0, 0]
    hcot = head_cot[0, 0]
    ws = (w_query[0], w_key[0], w_value[0])
    width = tok.shape[1]
    rows = tok.shape[0] + mem.shape[0]
    block = w_query.shape[1]
    quarter = block // 2
    qw = GROUP * HD
    cw = qw + 2 * HD
    z = lax.axis_index("seg")
    grp = lax.axis_index("grp")
    pair = z // 2
    inner = (z == 1) | (z == 2)
    partner = z + 1 - 2 * (z % 2)
    far_in = jnp.where(z < 2, 2, 1)
    far_out = jnp.where(z < 2, 3, 0)
    mine = grp * quarter
    theirs = (1 - grp) * quarter
    offsets = jnp.stack(
        [z * block]
        + [b * block + mine for b in (partner, far_out, far_in)]
        + [b * block + theirs for b in (partner, far_out, far_in)]
    ).astype(jnp.int32)
    places = jnp.stack(
        [
            pair * 2 * block,
            (1 - pair) * 2 * block,
            pair * block,
            (1 - pair) * block,
            grp,
            inner.astype(jnp.int32),
        ]
    ).astype(jnp.int32)

    smem = pl.BlockSpec(memory_space=pltpu.SMEM)
    vmem = pl.BlockSpec(memory_space=pltpu.VMEM)
    bf16 = jnp.bfloat16
    f32 = jnp.float32

    def shape(r, c, dtype=bf16):
        return jax.ShapeDtypeStruct((r, c), dtype)

    free = pl.CostEstimate(flops=0, bytes_accessed=0, transcendentals=0)
    anywhere = pl.BlockSpec(memory_space=pl.ANY)
    hbm = pl.BlockSpec(memory_space=pltpu.HBM)

    def part(r, c, at=0):
        return pl.BlockSpec((r, c), lambda *_: (0, at), pipeline_mode=pl.Buffered(1))

    def own_w(c):
        return [part(block, qw, c), part(block, HD, c), part(block, HD, c)]

    def call(kernel, outs, args, specs=None, mib=20, scratch=(), smems=1, aliases=None, out_specs=None):
        specs = specs or {}
        out_specs = out_specs or {}
        args = tuple(
            pltpu.with_memory_space_constraint(x, pltpu.HBM) if specs.get(k) is hbm else x
            for k, x in enumerate(args)
        )
        many = isinstance(outs, tuple)
        out_list = outs if many else (outs,)
        ins = [smem] * smems + [specs.get(k) or part(*args[k].shape) for k in range(smems, len(args))]
        ends = tuple(out_specs.get(k) or part(*o.shape) for k, o in enumerate(out_list))
        return pl.pallas_call(
            kernel,
            grid=(1,),
            out_shape=outs,
            in_specs=ins,
            out_specs=ends if many else ends[0],
            scratch_shapes=scratch,
            input_output_aliases=aliases or {},
            compiler_params=pltpu.CompilerParams(vmem_limit_bytes=mib * MIB),
            cost_estimate=free,
        )(*args)

    def permute(value, axis, route):
        return lax.ppermute(value, axis, route)

    def z_and(value):
        return jnp.concatenate(value, 0)

    order = Order(z.astype(jnp.int32))
    h01, h23 = call(
        halves_kernel,
        (shape(block, cw), shape(block, cw)),
        (places,) + ws,
        specs={k: hbm for k in (1, 2, 3)},
        scratch=[pltpu.SemaphoreType.DMA((12,))],
    )

    def head(i, pieces, starts, dn=()):
        args = (offsets, normed) + ws + tuple(pieces) + (hcot,)
        n = len(args)
        return call(
            functools.partial(head_kernel, i, starts),
            (shape(rows, cw), shape(rows, width, f32)),
            args + dn,
            specs={k: hbm for k in range(1, n)} | {6: anywhere},
            scratch=[
                pltpu.VMEM((width, cw), bf16),
                pltpu.VMEM((rows, width), bf16),
                pltpu.VMEM((rows, qw), bf16),
                pltpu.VMEM((rows, cw), bf16),
                pltpu.SemaphoreType.DMA((9,)),
            ],
            aliases={n: 1} if dn else None,
        )

    whole_shapes = tuple(shape(block, n * HEADS, f32) for n in (qw, HD, HD))

    def grads(i, n_t, ds, before, first=0, count=block, own=True):
        before = tuple(before) if own else ()
        args = (places, n_t) + tuple(ds) + before
        skip = 1 if count else 0
        outs = ((shape(count, cw),) if count else ()) + (whole_shapes if own else ())
        out = call(
            functools.partial(grads_kernel, first, count, own),
            outs,
            args,
            specs={6 + k: anywhere for k in range(len(before))},
            out_specs={skip + k: spec for k, spec in enumerate(own_w(i))} if own else None,
            scratch=[pltpu.VMEM((4 * rows, cw), bf16)],
            aliases={6 + k: skip + k for k in range(len(before))},
        )
        return (out[0] if count else None), out[skip:]

    def place(spots, recvs, before):
        n = 1 + len(spots)
        most = max(r.shape[0] for r in recvs)
        return call(
            functools.partial(place_kernel, spots),
            whole_shapes,
            (places,) + tuple(recvs) + tuple(before),
            specs={n + k: anywhere for k in range(3)},
            out_specs={k: anywhere for k in range(3)},
            scratch=[pltpu.VMEM((len(spots), most, w), f32) for w in (qw, HD, HD)]
            + [pltpu.SemaphoreType.DMA((len(spots), 3))],
            aliases={n + k: k for k in range(3)},
        )

    def pick(b, c):
        return jnp.where(inner, b, c)

    def send(d):
        return [permute(d, "seg", r) for r in (INWARD, FAR_INWARD, ACROSS)]

    a01 = permute(h01, "seg", SWAP)
    normed, near, far = call(
        functools.partial(normalise_kernel, 2 * block),
        (shape(rows, width), shape(rows, 2 * block), shape(rows, 2 * block)),
        (places, tok, mem, gain),
    )
    n_across = permute(far, "seg", ACROSS)
    a01, n_across, h01, h23, normed, near, far = order.point(
        a01, n_across, h01, h23, normed, near, far
    )
    a23 = permute(h23, "seg", SWAP)
    b0 = permute(z_and([a01[:quarter], h01[:quarter]]), "seg", ACROSS)
    ya01 = permute(a01, "grp", GRPS)
    to1 = z_and([a01[quarter:], h01[quarter:]])
    b0, ya01, a23, to1, h23, near, far = order.point(b0, ya01, a23, to1, h23, near, far)
    ya23 = permute(a23, "grp", GRPS)
    n_in = permute(near, "seg", INWARD)
    b1 = permute(to1, "seg", ACROSS)
    c0 = permute(b0, "seg", OUTWARD)
    to2 = z_and([a23[:quarter], h23[:quarter]])
    to3 = z_and([a23[quarter:], h23[quarter:]])
    f0 = pick(b0, c0)
    ya23, n_in, b1, f0, to2, to3, far = order.point(ya23, n_in, b1, f0, to2, to3, far)
    yf0 = permute(f0, "grp", GRPS)
    n_far = permute(far, "seg", FAR_INWARD)
    b2 = permute(to2, "seg", ACROSS)
    c1 = permute(b1, "seg", OUTWARD)
    f1 = pick(b1, c1)
    n_far, b2, f1, to3 = order.point(n_far, b2, f1, to3)
    yf1 = permute(f1, "grp", GRPS)
    b3 = permute(to3, "seg", ACROSS)
    c2 = permute(b2, "seg", OUTWARD)
    d0, dn = head(0, (a01, f0, ya01, yf0), (0, 0))
    f2 = pick(b2, c2)
    b3, f2, d0, dn = order.point(b3, f2, d0, dn)
    yf2 = permute(f2, "grp", GRPS)
    c3 = permute(b3, "seg", OUTWARD)
    x0 = send(d0)
    d1, dn = head(1, (a01, f1, ya01, yf1), (quarter, quarter), (dn,))
    n_t = call(
        turn_kernel,
        shape(2 * block, 4 * rows),
        (near, n_in, n_far, n_across),
        scratch=[pltpu.VMEM((4 * rows, 2 * block), bf16)],
        smems=0,
    )
    f3 = pick(b3, c3)
    f3, x00, x01, x02, d1, dn, n_t = order.point(f3, *x0, d1, dn, n_t)
    yf3 = permute(f3, "grp", GRPS)
    x1 = send(d1)
    o0, whole = grads(0, n_t, (d0, x00, x01, x02), ())
    r0 = permute(o0, "seg", OUTWARD)
    d2, dn = head(2, (a23, f2, ya23, yf2), (0, 0), (dn,))
    x10, x11, x12, d2, dn, o0 = order.point(*x1, d2, dn, o0)
    x2 = send(d2)
    o1, whole = grads(1, n_t, (d1, x10, x11, x12), whole)
    r1 = permute(o1, "seg", OUTWARD)
    d3, dn = head(3, (a23, f3, ya23, yf3), (quarter, quarter), (dn,))
    x20, x21, x22, d3, r0, dn, o1 = order.point(*x2, d3, r0, dn, o1)
    x3 = send(d3)
    parts2 = (d2, x20, x21, x22)
    o2, _ = grads(2, n_t, parts2, (), own=False)
    r2 = permute(o2, "seg", OUTWARD)
    half_rows = tok.shape[0] // 2
    token0, token1, memory_part, grad_g = call(
        rows_kernel,
        (shape(half_rows, width), shape(half_rows, width), shape(mem.shape[0], width), shape(1, width, f32)),
        (dn, tok, mem, gain, ocot),
        smems=0,
    )
    gains = lax.all_to_all(grad_g.reshape(4, width // 4), "seg", 0, 0, tiled=True)
    x30, x31, x32, r1, r2, token0, token1, memory_part, gains = order.point(
        *x3, r1, r2, token0, token1, memory_part, gains
    )
    parts3 = (d3, x30, x31, x32)
    o3, _ = grads(3, n_t, parts3, (), own=False)
    r3 = permute(o3, "seg", OUTWARD)
    below0, before = deliver(token0, memory_part)
    below1 = from_behind(token1, "section", -1)
    _, whole = grads(2, n_t, parts2, whole, count=0)
    _, whole = grads(3, n_t, parts3, whole, count=0)
    grad_gain = jnp.sum(gains, 0, keepdims=True)
    whole = place(((0, 0), (1, 0), (2, 0)), (r0, r1, r2), whole)
    below = call(copy_kernel, shape(tok.shape[0], width), (below0, below1), smems=0)
    r3, before, below, grad_gain, q_, k_, v_ = order.point(r3, before, below, grad_gain, *whole)
    grad_query, grad_key, grad_value = place(((3, 0),), (r3,), (q_, k_, v_))
    return (
        below[None, None],
        before[None, None],
        grad_query[None],
        grad_key[None],
        grad_value[None],
        grad_gain,
    )


def solution(mesh):
    in_specs = (
        P("section", ("grp", "seg"), None, None),
        P("section", ("grp", "seg"), None, None),
        P("section", ("grp", "seg"), None, None),
        P("section", ("grp", "seg"), None, None),
        P("section", "seg", None),
        P("section", "seg", None),
        P("section", "seg", None),
        P("section", None),
    )
    out_specs = (
        P("section", ("grp", "seg"), None, None),
        P("section", ("grp", "seg"), None, None),
        P(("grp", "section"), "seg", None),
        P(("grp", "section"), "seg", None),
        P(("grp", "section"), "seg", None),
        P(("grp", "section"), "seg"),
    )
    line = mesh.shape["seg"] == 4 and mesh.shape["grp"] == 2
    return jax.shard_map(
        on_line if line else on_device,
        mesh=mesh,
        in_specs=in_specs,
        out_specs=out_specs,
        check_vma=False,
    )
```

```python
import functools

import jax
import jax.numpy as jnp
from jax import lax
from jax.experimental import pallas as pl
from jax.experimental.pallas import tpu as pltpu
from jax.sharding import PartitionSpec as P

HEADS = 4
GROUP = 4
HD = 128
MIB = 1024 * 1024


def from_behind(block, axis, distance):
    devices = range(lax.axis_size(axis))
    route = [(i - distance, i) for i in devices if i - distance in devices]
    return lax.ppermute(block, axis, route)


def times_t(left, right):
    return lax.dot_general(
        left, right, (((1,), (1,)), ((), ())), preferred_element_type=jnp.float32
    )


def inner_rows(left, right):
    return lax.dot_general(
        left, right, (((0,), (0,)), ((), ())), preferred_element_type=jnp.float32
    )


def deliver(token_part, memory_part):
    below = from_behind(token_part, "section", -1)
    before = from_behind(memory_part, "seg", -1)
    return (below, before)


def on_device(inputs, memory, out_cot, head_cot, w_query, w_key, w_value, gain):
    whole_q, whole_k, whole_v = (
        lax.all_gather(w_query, "seg", axis=1, tiled=True),
        lax.all_gather(w_key, "seg", axis=1, tiled=True),
        lax.all_gather(w_value, "seg", axis=1, tiled=True),
    )
    wq = whole_q[0]
    wk = whole_k[0]
    wv = whole_v[0]
    tokens_in = inputs[0, 0]
    mem = memory[0, 0]
    ocot = out_cot[0, 0]
    hcot = head_cot[0, 0]
    gain_f = gain[0].astype(jnp.float32)
    mem_len = mem.shape[0]
    seg_len = tokens_in.shape[0]
    width = tokens_in.shape[1]
    query_width = wq.shape[1]
    rows = jnp.concatenate([mem, tokens_in, mem], 0)
    total = rows.shape[0]
    zf = rows.astype(jnp.float32)
    inv = lax.rsqrt(jnp.mean(zf * zf, -1, keepdims=True) + 1e-05)
    unit = zf * inv
    normed = (unit * gain_f).astype(jnp.bfloat16)
    query = (
        jnp.dot(normed, wq, preferred_element_type=jnp.float32)
        .astype(jnp.bfloat16)
        .reshape(total, HEADS, GROUP, HD)
    )
    keys = (
        jnp.dot(normed, wk, preferred_element_type=jnp.float32)
        .astype(jnp.bfloat16)
        .reshape(total, HEADS, HD)
    )
    values = (
        jnp.dot(normed, wv, preferred_element_type=jnp.float32)
        .astype(jnp.bfloat16)
        .reshape(total, HEADS, HD)
    )
    scale = HD ** (-0.5)
    scores = jnp.einsum("qhgd,khd->hgqk", query, keys, preferred_element_type=jnp.float32) * scale
    places = jnp.arange(total)
    causal = places[:, None] >= places[None, :]
    scores = jnp.where(causal[None, None], scores, -1e30)
    probs = jax.nn.softmax(scores, -1)
    probs_b = probs.astype(jnp.bfloat16)
    cot = jnp.concatenate([jnp.zeros((mem_len, width), jnp.bfloat16), ocot], 0)
    d_attn = jnp.concatenate([jnp.zeros((mem_len, query_width), jnp.bfloat16), hcot], 0)
    d_heads = d_attn.reshape(total, HEADS, GROUP, HD)
    d_probs = jnp.einsum("qhgd,khd->hgqk", d_heads, values, preferred_element_type=jnp.float32)
    d_scores = (probs * (d_probs - jnp.sum(probs * d_probs, -1, keepdims=True)) * scale).astype(
        jnp.bfloat16
    )
    d_values = jnp.einsum("hgqk,qhgd->khd", probs_b, d_heads, preferred_element_type=jnp.float32)
    d_values = d_values.astype(jnp.bfloat16).reshape(total, HEADS * HD)
    d_query = jnp.einsum("hgqk,khd->qhgd", d_scores, keys, preferred_element_type=jnp.float32)
    d_query = d_query.astype(jnp.bfloat16).reshape(total, query_width)
    d_keys = jnp.einsum("hgqk,qhgd->khd", d_scores, query, preferred_element_type=jnp.float32)
    d_keys = d_keys.astype(jnp.bfloat16).reshape(total, HEADS * HD)
    d_normed = times_t(d_query, wq) + times_t(d_keys, wk) + times_t(d_values, wv)
    grad_g = jnp.sum(d_normed * unit, 0)
    d_unit = d_normed * gain_f
    d_rows = cot.astype(jnp.float32) + inv * (
        d_unit - unit * jnp.mean(d_unit * unit, -1, keepdims=True)
    )
    token_part = d_rows[mem_len : mem_len + seg_len].astype(jnp.bfloat16)
    memory_part = (d_rows[:mem_len] + d_rows[mem_len + seg_len :]).astype(jnp.bfloat16)
    grad_q = inner_rows(normed, d_query)
    grad_k = inner_rows(normed, d_keys)
    grad_v = inner_rows(normed, d_values)
    grad_query, grad_key, grad_value = (
        lax.psum_scatter(
            grad_q[None].astype(jnp.bfloat16), "seg", scatter_dimension=1, tiled=True
        ).astype(jnp.float32),
        lax.psum_scatter(
            grad_k[None].astype(jnp.bfloat16), "seg", scatter_dimension=1, tiled=True
        ).astype(jnp.float32),
        lax.psum_scatter(
            grad_v[None].astype(jnp.bfloat16), "seg", scatter_dimension=1, tiled=True
        ).astype(jnp.float32),
    )
    grad_gain = lax.psum_scatter(grad_g[None], "seg", scatter_dimension=1, tiled=True)
    below, before = deliver(token_part, memory_part)
    return (below[None, None], before[None, None], grad_query, grad_key, grad_value, grad_gain)


SWAP = [(0, 1), (1, 0), (2, 3), (3, 2)]
ACROSS = [(1, 2), (2, 1)]
OUTWARD = [(1, 0), (2, 3)]
INWARD = [(0, 1), (3, 2)]
FAR_INWARD = [(0, 2), (3, 1)]
GRPS = [(0, 1), (1, 0)]


def normalise_kernel(half, place_ref, tok_ref, mem_ref, gain_ref, n_ref, near_ref, far_ref):
    seg_len = tok_ref.shape[0]
    gain = gain_ref[...].astype(jnp.float32)

    def piece(rows):
        zf = rows.astype(jnp.float32)
        inv = lax.rsqrt(jnp.mean(zf * zf, -1, keepdims=True) + 1e-05)
        return (zf * inv * gain).astype(jnp.bfloat16)

    step = 32

    @pl.loop(0, seg_len // step)
    def _(i):
        at = pl.ds(pl.multiple_of(i * step, step), step)
        n_ref[at, :] = piece(tok_ref[at, :])

    n_ref[seg_len:, :] = piece(mem_ref[...])
    near = pl.multiple_of(place_ref[0], 128)
    far = pl.multiple_of(place_ref[1], 128)
    near_ref[...] = n_ref[:, pl.ds(near, half)]
    far_ref[...] = n_ref[:, pl.ds(far, half)]


def halves_kernel(place_ref, wq, wk, wv, first, second, sems):
    quarter = first.shape[0] // 2
    qw = GROUP * HD
    at = pl.ds(pl.multiple_of(place_ref[4] * quarter, quarter), quarter)
    copies = []
    for c in range(HEADS):
        out = (first, second)[c // 2]
        to = slice((c % 2) * quarter, (c % 2 + 1) * quarter)
        for k, (w, start, wide) in enumerate(((wq, 0, qw), (wk, qw, HD), (wv, qw + HD, HD))):
            copies.append(
                pltpu.make_async_copy(
                    w.at[at, c * wide : (c + 1) * wide],
                    out.at[to, start : start + wide],
                    sems.at[3 * c + k],
                )
            )
    for copy in copies:
        copy.start()
    for copy in copies:
        copy.wait()


def fetch(copies):
    copies = [pltpu.make_async_copy(*c) for c in copies]
    for copy in copies:
        copy.start()
    return copies


def weight_copies(refs, starts, c, w_ref, sems):
    wq, wk, wv, a, far, ya, yfar = refs
    block = wq.shape[0]
    quarter = block // 2
    qw = GROUP * HD
    sources = [
        (wq.at[:, c * qw : (c + 1) * qw], slice(0, block), slice(0, qw)),
        (wk.at[:, c * HD : (c + 1) * HD], slice(0, block), slice(qw, qw + HD)),
        (wv.at[:, c * HD : (c + 1) * HD], slice(0, block), slice(qw + HD, qw + 2 * HD)),
    ]
    at = block
    for ref, start, rows in (
        (a, starts[0], quarter),
        (far, 0, 2 * quarter),
        (ya, starts[1], quarter),
        (yfar, 0, 2 * quarter),
    ):
        sources.append(
            (ref.at[start : start + rows, :], slice(at, at + rows), slice(0, w_ref.shape[1]))
        )
        at += rows
    return [(src, w_ref.at[r, k], sems.at[n]) for n, (src, r, k) in enumerate(sources)]


def piece_rows(block):
    quarter = block // 2
    sizes = [block] + [quarter] * 6
    waits = [(0, 1, 2), (3,), (4,), (), (5,), (6,), ()]
    at = 0
    for size, wait in zip(sizes, waits):
        yield at, size, wait
        at += size


def head_kernel(c, starts, off_ref, n_hbm, wq, wk, wv, a, far, ya, yfar, hcot_hbm, *refs):
    d_ref, dn_ref, w_ref, n_ref, h_ref, qkv_ref, sems = refs[-7:]
    rows = n_ref.shape[0]
    qw = GROUP * HD
    first = fetch([(n_hbm, n_ref, sems.at[7])])[0]
    copies = fetch(weight_copies((wq, wk, wv, a, far, ya, yfar), starts, c, w_ref, sems))
    cots = fetch([(hcot_hbm.at[:, c * qw : (c + 1) * qw], h_ref, sems.at[8])])[0]
    first.wait()
    total = None
    for i, (start, count, waits) in enumerate(piece_rows(wq.shape[0])):
        for k in waits:
            copies[k].wait()
        at = pl.ds(pl.multiple_of(off_ref[i], 128), count)
        part = jnp.dot(
            n_ref[:, at], w_ref[start : start + count, :], preferred_element_type=jnp.float32
        )
        total = part if total is None else total + part
    qkv_ref[...] = total.astype(jnp.bfloat16)
    cots.wait()
    mem = rows - (rows // 128) * 128
    seg_len = rows - mem
    keys = jnp.concatenate([qkv_ref[:, qw : qw + HD], qkv_ref[seg_len:, qw : qw + HD]], 0)
    values = jnp.concatenate([qkv_ref[:, qw + HD :], qkv_ref[seg_len:, qw + HD :]], 0)
    scale = HD ** (-0.5)
    wide = rows + mem
    row = lax.broadcasted_iota(jnp.int32, (rows, wide), 0)
    col = lax.broadcasted_iota(jnp.int32, (rows, wide), 1)
    need = jnp.where(col < seg_len, col, jnp.where(col < rows, 0, col - mem))
    seen = row >= need
    d_keys = None
    d_values = None
    for g in range(GROUP):
        q = qkv_ref[:, g * HD : (g + 1) * HD]
        da = h_ref[:, g * HD : (g + 1) * HD]
        s = jnp.where(seen, times_t(q, keys) * scale, -1e30)
        e = jnp.exp(s - jnp.max(s, -1, keepdims=True))
        p = e / jnp.sum(e, -1, keepdims=True)
        dp = times_t(da, values)
        ds = (p * (dp - jnp.sum(p * dp, -1, keepdims=True)) * scale).astype(jnp.bfloat16)
        d_ref[:, g * HD : (g + 1) * HD] = jnp.dot(
            ds, keys, preferred_element_type=jnp.float32
        ).astype(jnp.bfloat16)
        dk = inner_rows(ds, q)
        dv = inner_rows(p.astype(jnp.bfloat16), da)
        d_keys = dk if d_keys is None else d_keys + dk
        d_values = dv if d_values is None else d_values + dv
    for at, both in ((qw, d_keys), (qw + HD, d_values)):
        d_ref[:seg_len, at : at + HD] = both[:seg_len].astype(jnp.bfloat16)
        d_ref[seg_len:, at : at + HD] = (both[seg_len:rows] + both[rows:]).astype(jnp.bfloat16)
    for i, (start, count, _) in enumerate(piece_rows(wq.shape[0])):
        at = pl.ds(pl.multiple_of(off_ref[i], 128), count)
        part = times_t(d_ref[...], w_ref[start : start + count, :])
        dn_ref[:, at] = refs[0][:, at] + part if len(refs) > 7 else part


def rows_kernel(dn_ref, tok_ref, mem_ref, gain_ref, cot_ref, token0, token1, memory_ref, gg_ref):
    seg_len = tok_ref.shape[0]
    gain = gain_ref[...].astype(jnp.float32)
    step = mem_ref.shape[0]

    def piece(rows, dn, cot):
        zf = rows.astype(jnp.float32)
        inv = lax.rsqrt(jnp.mean(zf * zf, -1, keepdims=True) + 1e-05)
        unit = zf * inv
        gg_ref[...] += jnp.sum(dn * unit, 0, keepdims=True)
        du = dn * gain
        out = cot.astype(jnp.float32) + inv * (
            du - unit * jnp.mean(du * unit, -1, keepdims=True)
        )
        return out.astype(jnp.bfloat16)

    gg_ref[...] = jnp.zeros_like(gg_ref)

    for k, token_ref in enumerate((token0, token1)):

        @pl.loop(0, seg_len // 2 // step)
        def _(i, token_ref=token_ref, k=k):
            to = pl.ds(pl.multiple_of(i * step, step), step)
            at = pl.ds(pl.multiple_of(k * seg_len // 2 + i * step, step), step)
            token_ref[to, :] = piece(tok_ref[at, :], dn_ref[at, :], cot_ref[at, :])

    memory_ref[...] = piece(mem_ref[...], dn_ref[seg_len:, :], cot_ref[seg_len:, :])


def turn_kernel(n0, n1, n2, n3, out_ref, cat_ref, sems):
    rows = n0.shape[0]
    copies = fetch(
        [
            (ref, cat_ref.at[i * rows : (i + 1) * rows, :], sems.at[i])
            for i, ref in enumerate((n0, n1, n2, n3))
        ]
    )
    for copy in copies:
        copy.wait()
    for i in range(out_ref.shape[0] // 256):
        at = slice(256 * i, 256 * (i + 1))
        out_ref[at, :] = cat_ref[:, at].T


def grads_kernel(first, count, own, place_ref, nt_ref, d0, d1, d2, d3, *refs):
    dcat_ref = refs[-1]
    outs = refs[-4 - (count > 0) : -1] if own else refs[-2:-1]

    @pl.when(place_ref[5] == 1)
    def _():
        rows = d0.shape[0]
        for i, ref in enumerate((d0, d1, d2, d3)):
            dcat_ref[i * rows : (i + 1) * rows, :] = ref[...]
        block = nt_ref.shape[0] // 2
        qw = GROUP * HD
        if count:
            other = pl.ds(pl.multiple_of(place_ref[2] + first, 128), count)
            outs[0][...] = jnp.dot(
                nt_ref[other, :], dcat_ref[...], preferred_element_type=jnp.float32
            ).astype(jnp.bfloat16)
        if own:
            mine = pl.ds(pl.multiple_of(place_ref[3], 128), block)
            q_ref, k_ref, v_ref = outs[-3:]
            total = jnp.dot(nt_ref[mine, :], dcat_ref[...], preferred_element_type=jnp.float32)
            q_ref[...] = total[:, :qw]
            k_ref[...] = total[:, qw : qw + HD]
            v_ref[...] = total[:, qw + HD :]


def place_kernel(spots, place_ref, *refs):
    recvs = refs[: len(spots)]
    q_ref, k_ref, v_ref, q_buf, k_buf, v_buf, sems = refs[len(spots) + 3 : len(spots) + 10]
    held = refs[len(spots) + 10 :]
    qw = GROUP * HD

    @pl.when(place_ref[5] == 0)
    def _():
        waiting = []
        if held:
            coming = fetch([(recv, held[0].at[n], held[1].at[n]) for n, recv in enumerate(recvs)])
        for n, ((c, first), recv) in enumerate(zip(spots, recvs)):
            count = recv.shape[0]
            if held:
                coming[n].wait()
                recv = held[0].at[n]
            for k, (buf, ref, at, wide) in enumerate(
                ((q_buf, q_ref, 0, qw), (k_buf, k_ref, qw, HD), (v_buf, v_ref, qw + HD, HD))
            ):
                buf[n, :count, :] = recv[:, at : at + wide].astype(jnp.float32)
                copy = pltpu.make_async_copy(
                    buf.at[n, :count, :],
                    ref.at[first : first + count, c * wide : (c + 1) * wide],
                    sems.at[n, k],
                )
                copy.start()
                waiting.append(copy)
        for copy in waiting:
            copy.wait()


def copy_kernel(*refs):
    out_ref = refs[-1]
    at = 0
    for ref in refs[:-1]:
        out_ref[at : at + ref.shape[0], :] = ref[...]
        at += ref.shape[0]


class Order:
    def __init__(self, mark):
        self.mark = mark

    def point(self, *values):
        out = lax.optimization_barrier((self.mark,) + values)
        self.mark = out[0]
        return out[1] if len(values) == 1 else out[1:]


def on_line(inputs, memory, out_cot, head_cot, w_query, w_key, w_value, gain):
    tok = inputs[0, 0]
    mem = memory[0, 0]
    ocot = out_cot[0, 0]
    hcot = head_cot[0, 0]
    ws = (w_query[0], w_key[0], w_value[0])
    width = tok.shape[1]
    rows = tok.shape[0] + mem.shape[0]
    block = w_query.shape[1]
    quarter = block // 2
    qw = GROUP * HD
    cw = qw + 2 * HD
    z = lax.axis_index("seg")
    grp = lax.axis_index("grp")
    pair = z // 2
    inner = (z == 1) | (z == 2)
    partner = z + 1 - 2 * (z % 2)
    far_in = jnp.where(z < 2, 2, 1)
    far_out = jnp.where(z < 2, 3, 0)
    mine = grp * quarter
    theirs = (1 - grp) * quarter
    offsets = jnp.stack(
        [z * block]
        + [b * block + mine for b in (partner, far_out, far_in)]
        + [b * block + theirs for b in (partner, far_out, far_in)]
    ).astype(jnp.int32)
    places = jnp.stack(
        [
            pair * 2 * block,
            (1 - pair) * 2 * block,
            pair * block,
            (1 - pair) * block,
            grp,
            inner.astype(jnp.int32),
        ]
    ).astype(jnp.int32)

    smem = pl.BlockSpec(memory_space=pltpu.SMEM)
    vmem = pl.BlockSpec(memory_space=pltpu.VMEM)
    bf16 = jnp.bfloat16
    f32 = jnp.float32

    def shape(r, c, dtype=bf16):
        return jax.ShapeDtypeStruct((r, c), dtype)

    free = pl.CostEstimate(flops=0, bytes_accessed=0, transcendentals=0)
    anywhere = pl.BlockSpec(memory_space=pl.ANY)
    hbm = pl.BlockSpec(memory_space=pltpu.HBM)

    def part(r, c, at=0):
        return pl.BlockSpec((r, c), lambda *_: (0, at), pipeline_mode=pl.Buffered(1))

    def own_w(c):
        return [part(block, qw, c), part(block, HD, c), part(block, HD, c)]

    def call(kernel, outs, args, specs=None, mib=20, scratch=(), smems=1, aliases=None, out_specs=None):
        specs = specs or {}
        out_specs = out_specs or {}
        args = tuple(
            pltpu.with_memory_space_constraint(x, pltpu.HBM) if specs.get(k) is hbm else x
            for k, x in enumerate(args)
        )
        many = isinstance(outs, tuple)
        out_list = outs if many else (outs,)
        ins = [smem] * smems + [specs.get(k) or part(*args[k].shape) for k in range(smems, len(args))]
        ends = tuple(out_specs.get(k) or part(*o.shape) for k, o in enumerate(out_list))
        return pl.pallas_call(
            kernel,
            grid=(1,),
            out_shape=outs,
            in_specs=ins,
            out_specs=ends if many else ends[0],
            scratch_shapes=scratch,
            input_output_aliases=aliases or {},
            compiler_params=pltpu.CompilerParams(vmem_limit_bytes=mib * MIB),
            cost_estimate=free,
        )(*args)

    def permute(value, axis, route):
        return lax.ppermute(value, axis, route)

    def z_and(value):
        return jnp.concatenate(value, 0)

    order = Order(z.astype(jnp.int32))
    h01, h23 = call(
        halves_kernel,
        (shape(block, cw), shape(block, cw)),
        (places,) + ws,
        specs={k: hbm for k in (1, 2, 3)},
        scratch=[pltpu.SemaphoreType.DMA((12,))],
    )

    def head(i, pieces, starts, dn=()):
        args = (offsets, normed) + ws + tuple(pieces) + (hcot,)
        n = len(args)
        return call(
            functools.partial(head_kernel, i, starts),
            (shape(rows, cw), shape(rows, width, f32)),
            args + dn,
            specs={k: hbm for k in range(1, n)} | {6: anywhere},
            scratch=[
                pltpu.VMEM((width, cw), bf16),
                pltpu.VMEM((rows, width), bf16),
                pltpu.VMEM((rows, qw), bf16),
                pltpu.VMEM((rows, cw), bf16),
                pltpu.SemaphoreType.DMA((9,)),
            ],
            aliases={n: 1} if dn else None,
        )

    whole_shapes = tuple(shape(block, n * HEADS, f32) for n in (qw, HD, HD))

    def grads(i, n_t, ds, before, first=0, count=block, own=True):
        before = tuple(before) if own else ()
        args = (places, n_t) + tuple(ds) + before
        skip = 1 if count else 0
        outs = ((shape(count, cw),) if count else ()) + (whole_shapes if own else ())
        out = call(
            functools.partial(grads_kernel, first, count, own),
            outs,
            args,
            specs={6 + k: anywhere for k in range(len(before))},
            out_specs={skip + k: spec for k, spec in enumerate(own_w(i))} if own else None,
            scratch=[pltpu.VMEM((4 * rows, cw), bf16)],
            aliases={6 + k: skip + k for k in range(len(before))},
        )
        return (out[0] if count else None), out[skip:]

    def place(spots, recvs, before, from_hbm=False):
        n = 1 + len(spots)
        most = max(r.shape[0] for r in recvs)
        return call(
            functools.partial(place_kernel, spots),
            whole_shapes,
            (places,) + tuple(recvs) + tuple(before),
            specs={n + k: anywhere for k in range(3)}
            | ({1 + k: hbm for k in range(len(spots))} if from_hbm else {}),
            out_specs={k: anywhere for k in range(3)},
            scratch=[pltpu.VMEM((len(spots), most, w), f32) for w in (qw, HD, HD)]
            + [pltpu.SemaphoreType.DMA((len(spots), 3))]
            + (
                [
                    pltpu.VMEM((len(spots), most, cw), bf16),
                    pltpu.SemaphoreType.DMA((len(spots),)),
                ]
                if from_hbm
                else []
            ),
            aliases={n + k: k for k in range(3)},
        )

    def pick(b, c):
        return jnp.where(inner, b, c)

    def send(d):
        return [permute(d, "seg", r) for r in (INWARD, FAR_INWARD, ACROSS)]

    a01 = permute(h01, "seg", SWAP)
    normed, near, far = call(
        functools.partial(normalise_kernel, 2 * block),
        (shape(rows, width), shape(rows, 2 * block), shape(rows, 2 * block)),
        (places, tok, mem, gain),
    )
    n_across = permute(far, "seg", ACROSS)
    a01, n_across, h01, h23, normed, near, far = order.point(
        a01, n_across, h01, h23, normed, near, far
    )
    a23 = permute(h23, "seg", SWAP)
    b0 = permute(z_and([a01[:quarter], h01[:quarter]]), "seg", ACROSS)
    ya01 = permute(a01, "grp", GRPS)
    to1 = z_and([a01[quarter:], h01[quarter:]])
    b0, ya01, a23, to1, h23, near, far = order.point(b0, ya01, a23, to1, h23, near, far)
    b1 = permute(to1, "seg", ACROSS)
    c0 = permute(b0, "seg", OUTWARD)
    to2 = z_and([a23[:quarter], h23[:quarter]])
    to3 = z_and([a23[quarter:], h23[quarter:]])
    f0 = pick(b0, c0)
    b1, f0, to2, to3, a23, near, far = order.point(b1, f0, to2, to3, a23, near, far)
    yf0 = permute(f0, "grp", GRPS)
    ya23 = permute(a23, "grp", GRPS)
    n_far = permute(far, "seg", FAR_INWARD)
    b2 = permute(to2, "seg", ACROSS)
    c1 = permute(b1, "seg", OUTWARD)
    f1 = pick(b1, c1)
    n_far, b2, f1, to3, ya23, near = order.point(n_far, b2, f1, to3, ya23, near)
    yf1 = permute(f1, "grp", GRPS)
    n_in = permute(near, "seg", INWARD)
    b3 = permute(to3, "seg", ACROSS)
    c2 = permute(b2, "seg", OUTWARD)
    d0, dn = head(0, (a01, f0, ya01, yf0), (0, 0))
    f2 = pick(b2, c2)
    b3, f2, d0, dn, n_in = order.point(b3, f2, d0, dn, n_in)
    yf2 = permute(f2, "grp", GRPS)
    c3 = permute(b3, "seg", OUTWARD)
    x0 = send(d0)
    d1, dn = head(1, (a01, f1, ya01, yf1), (quarter, quarter), (dn,))
    n_t = call(
        turn_kernel,
        shape(2 * block, 4 * rows),
        (near, n_in, n_far, n_across),
        specs={k: hbm for k in range(4)},
        scratch=[pltpu.VMEM((4 * rows, 2 * block), bf16), pltpu.SemaphoreType.DMA((4,))],
        smems=0,
    )
    f3 = pick(b3, c3)
    f3, x00, x01, x02, d1, dn, n_t = order.point(f3, *x0, d1, dn, n_t)
    yf3 = permute(f3, "grp", GRPS)
    x1 = send(d1)
    o0, whole = grads(0, n_t, (d0, x00, x01, x02), ())
    r0 = permute(o0, "seg", OUTWARD)
    d2, dn = head(2, (a23, f2, ya23, yf2), (0, 0), (dn,))
    x10, x11, x12, d2, dn, o0 = order.point(*x1, d2, dn, o0)
    x2 = send(d2)
    o1, whole = grads(1, n_t, (d1, x10, x11, x12), whole)
    r1 = permute(o1, "seg", OUTWARD)
    d3, dn = head(3, (a23, f3, ya23, yf3), (quarter, quarter), (dn,))
    x20, x21, x22, d3, r0, dn, o1 = order.point(*x2, d3, r0, dn, o1)
    x3 = send(d3)
    parts2 = (d2, x20, x21, x22)
    o2, _ = grads(2, n_t, parts2, (), own=False)
    r2 = permute(o2, "seg", OUTWARD)
    half_rows = tok.shape[0] // 2
    token0, token1, memory_part, grad_g = call(
        rows_kernel,
        (shape(half_rows, width), shape(half_rows, width), shape(mem.shape[0], width), shape(1, width, f32)),
        (dn, tok, mem, gain, ocot),
        smems=0,
    )
    gains = lax.all_to_all(grad_g.reshape(4, width // 4), "seg", 0, 0, tiled=True)
    x30, x31, x32, r1, r2, token0, token1, memory_part, gains = order.point(
        *x3, r1, r2, token0, token1, memory_part, gains
    )
    parts3 = (d3, x30, x31, x32)
    o3, _ = grads(3, n_t, parts3, (), own=False)
    r3 = permute(o3, "seg", OUTWARD)
    below0, before = deliver(token0, memory_part)
    below1 = from_behind(token1, "section", -1)
    _, whole = grads(2, n_t, parts2, whole, count=0)
    _, whole = grads(3, n_t, parts3, whole, count=0)
    grad_gain = jnp.sum(gains, 0, keepdims=True)
    whole = place(((0, 0), (1, 0), (2, 0)), (r0, r1, r2), whole, True)
    below = call(copy_kernel, shape(tok.shape[0], width), (below0, below1), smems=0)
    r3, before, below, grad_gain, q_, k_, v_ = order.point(r3, before, below, grad_gain, *whole)
    grad_query, grad_key, grad_value = place(((3, 0),), (r3,), (q_, k_, v_))
    return (
        below[None, None],
        before[None, None],
        grad_query[None],
        grad_key[None],
        grad_value[None],
        grad_gain,
    )


def solution(mesh):
    in_specs = (
        P("section", ("grp", "seg"), None, None),
        P("section", ("grp", "seg"), None, None),
        P("section", ("grp", "seg"), None, None),
        P("section", ("grp", "seg"), None, None),
        P("section", "seg", None),
        P("section", "seg", None),
        P("section", "seg", None),
        P("section", None),
    )
    out_specs = (
        P("section", ("grp", "seg"), None, None),
        P("section", ("grp", "seg"), None, None),
        P(("grp", "section"), "seg", None),
        P(("grp", "section"), "seg", None),
        P(("grp", "section"), "seg", None),
        P(("grp", "section"), "seg"),
    )
    line = mesh.shape["seg"] == 4 and mesh.shape["grp"] == 2
    return jax.shard_map(
        on_line if line else on_device,
        mesh=mesh,
        in_specs=in_specs,
        out_specs=out_specs,
        check_vma=False,
    )
```

```python
import functools

import jax
import jax.numpy as jnp
from jax import lax
from jax.experimental import pallas as pl
from jax.experimental.pallas import tpu as pltpu
from jax.sharding import PartitionSpec as P

HEADS = 4
GROUP = 4
HD = 128
MIB = 1024 * 1024


def from_behind(block, axis, distance):
    devices = range(lax.axis_size(axis))
    route = [(i - distance, i) for i in devices if i - distance in devices]
    return lax.ppermute(block, axis, route)


def times_t(left, right):
    return lax.dot_general(
        left, right, (((1,), (1,)), ((), ())), preferred_element_type=jnp.float32
    )


def inner_rows(left, right):
    return lax.dot_general(
        left, right, (((0,), (0,)), ((), ())), preferred_element_type=jnp.float32
    )


def deliver(token_part, memory_part):
    below = from_behind(token_part, "section", -1)
    before = from_behind(memory_part, "seg", -1)
    return (below, before)


def on_device(inputs, memory, out_cot, head_cot, w_query, w_key, w_value, gain):
    whole_q, whole_k, whole_v = (
        lax.all_gather(w_query, "seg", axis=1, tiled=True),
        lax.all_gather(w_key, "seg", axis=1, tiled=True),
        lax.all_gather(w_value, "seg", axis=1, tiled=True),
    )
    wq = whole_q[0]
    wk = whole_k[0]
    wv = whole_v[0]
    tokens_in = inputs[0, 0]
    mem = memory[0, 0]
    ocot = out_cot[0, 0]
    hcot = head_cot[0, 0]
    gain_f = gain[0].astype(jnp.float32)
    mem_len = mem.shape[0]
    seg_len = tokens_in.shape[0]
    width = tokens_in.shape[1]
    query_width = wq.shape[1]
    rows = jnp.concatenate([mem, tokens_in, mem], 0)
    total = rows.shape[0]
    zf = rows.astype(jnp.float32)
    inv = lax.rsqrt(jnp.mean(zf * zf, -1, keepdims=True) + 1e-05)
    unit = zf * inv
    normed = (unit * gain_f).astype(jnp.bfloat16)
    query = (
        jnp.dot(normed, wq, preferred_element_type=jnp.float32)
        .astype(jnp.bfloat16)
        .reshape(total, HEADS, GROUP, HD)
    )
    keys = (
        jnp.dot(normed, wk, preferred_element_type=jnp.float32)
        .astype(jnp.bfloat16)
        .reshape(total, HEADS, HD)
    )
    values = (
        jnp.dot(normed, wv, preferred_element_type=jnp.float32)
        .astype(jnp.bfloat16)
        .reshape(total, HEADS, HD)
    )
    scale = HD ** (-0.5)
    scores = jnp.einsum("qhgd,khd->hgqk", query, keys, preferred_element_type=jnp.float32) * scale
    places = jnp.arange(total)
    causal = places[:, None] >= places[None, :]
    scores = jnp.where(causal[None, None], scores, -1e30)
    probs = jax.nn.softmax(scores, -1)
    probs_b = probs.astype(jnp.bfloat16)
    cot = jnp.concatenate([jnp.zeros((mem_len, width), jnp.bfloat16), ocot], 0)
    d_attn = jnp.concatenate([jnp.zeros((mem_len, query_width), jnp.bfloat16), hcot], 0)
    d_heads = d_attn.reshape(total, HEADS, GROUP, HD)
    d_probs = jnp.einsum("qhgd,khd->hgqk", d_heads, values, preferred_element_type=jnp.float32)
    d_scores = (probs * (d_probs - jnp.sum(probs * d_probs, -1, keepdims=True)) * scale).astype(
        jnp.bfloat16
    )
    d_values = jnp.einsum("hgqk,qhgd->khd", probs_b, d_heads, preferred_element_type=jnp.float32)
    d_values = d_values.astype(jnp.bfloat16).reshape(total, HEADS * HD)
    d_query = jnp.einsum("hgqk,khd->qhgd", d_scores, keys, preferred_element_type=jnp.float32)
    d_query = d_query.astype(jnp.bfloat16).reshape(total, query_width)
    d_keys = jnp.einsum("hgqk,qhgd->khd", d_scores, query, preferred_element_type=jnp.float32)
    d_keys = d_keys.astype(jnp.bfloat16).reshape(total, HEADS * HD)
    d_normed = times_t(d_query, wq) + times_t(d_keys, wk) + times_t(d_values, wv)
    grad_g = jnp.sum(d_normed * unit, 0)
    d_unit = d_normed * gain_f
    d_rows = cot.astype(jnp.float32) + inv * (
        d_unit - unit * jnp.mean(d_unit * unit, -1, keepdims=True)
    )
    token_part = d_rows[mem_len : mem_len + seg_len].astype(jnp.bfloat16)
    memory_part = (d_rows[:mem_len] + d_rows[mem_len + seg_len :]).astype(jnp.bfloat16)
    grad_q = inner_rows(normed, d_query)
    grad_k = inner_rows(normed, d_keys)
    grad_v = inner_rows(normed, d_values)
    grad_query, grad_key, grad_value = (
        lax.psum_scatter(
            grad_q[None].astype(jnp.bfloat16), "seg", scatter_dimension=1, tiled=True
        ).astype(jnp.float32),
        lax.psum_scatter(
            grad_k[None].astype(jnp.bfloat16), "seg", scatter_dimension=1, tiled=True
        ).astype(jnp.float32),
        lax.psum_scatter(
            grad_v[None].astype(jnp.bfloat16), "seg", scatter_dimension=1, tiled=True
        ).astype(jnp.float32),
    )
    grad_gain = lax.psum_scatter(grad_g[None], "seg", scatter_dimension=1, tiled=True)
    below, before = deliver(token_part, memory_part)
    return (below[None, None], before[None, None], grad_query, grad_key, grad_value, grad_gain)


SWAP = [(0, 1), (1, 0), (2, 3), (3, 2)]
ACROSS = [(1, 2), (2, 1)]
OUTWARD = [(1, 0), (2, 3)]
INWARD = [(0, 1), (3, 2)]
FAR_INWARD = [(0, 2), (3, 1)]
GRPS = [(0, 1), (1, 0)]


def normalise_kernel(half, place_ref, tok_ref, mem_ref, gain_ref, n_ref, near_ref, far_ref):
    seg_len = tok_ref.shape[0]
    gain = gain_ref[...].astype(jnp.float32)

    def piece(rows):
        zf = rows.astype(jnp.float32)
        inv = lax.rsqrt(jnp.mean(zf * zf, -1, keepdims=True) + 1e-05)
        return (zf * inv * gain).astype(jnp.bfloat16)

    step = 32

    @pl.loop(0, seg_len // step)
    def _(i):
        at = pl.ds(pl.multiple_of(i * step, step), step)
        n_ref[at, :] = piece(tok_ref[at, :])

    n_ref[seg_len:, :] = piece(mem_ref[...])
    near = pl.multiple_of(place_ref[0], 128)
    far = pl.multiple_of(place_ref[1], 128)
    near_ref[...] = n_ref[:, pl.ds(near, half)]
    far_ref[...] = n_ref[:, pl.ds(far, half)]


def halves_kernel(place_ref, wq, wk, wv, first, second, sems):
    quarter = first.shape[0] // 2
    qw = GROUP * HD
    at = pl.ds(pl.multiple_of(place_ref[4] * quarter, quarter), quarter)
    copies = []
    for c in range(HEADS):
        out = (first, second)[c // 2]
        to = slice((c % 2) * quarter, (c % 2 + 1) * quarter)
        for k, (w, start, wide) in enumerate(((wq, 0, qw), (wk, qw, HD), (wv, qw + HD, HD))):
            copies.append(
                pltpu.make_async_copy(
                    w.at[at, c * wide : (c + 1) * wide],
                    out.at[to, start : start + wide],
                    sems.at[3 * c + k],
                )
            )
    for copy in copies:
        copy.start()
    for copy in copies:
        copy.wait()


def fetch(copies):
    copies = [pltpu.make_async_copy(*c) for c in copies]
    for copy in copies:
        copy.start()
    return copies


def weight_copies(refs, starts, c, w_ref, sems):
    wq, wk, wv, a, far, ya, yfar = refs
    block = wq.shape[0]
    quarter = block // 2
    qw = GROUP * HD
    sources = [
        (wq.at[:, c * qw : (c + 1) * qw], slice(0, block), slice(0, qw)),
        (wk.at[:, c * HD : (c + 1) * HD], slice(0, block), slice(qw, qw + HD)),
        (wv.at[:, c * HD : (c + 1) * HD], slice(0, block), slice(qw + HD, qw + 2 * HD)),
    ]
    at = block
    for ref, start, rows in (
        (a, starts[0], quarter),
        (far, 0, 2 * quarter),
        (ya, starts[1], quarter),
        (yfar, 0, 2 * quarter),
    ):
        sources.append(
            (ref.at[start : start + rows, :], slice(at, at + rows), slice(0, w_ref.shape[1]))
        )
        at += rows
    return [(src, w_ref.at[r, k], sems.at[n]) for n, (src, r, k) in enumerate(sources)]


def piece_rows(block):
    quarter = block // 2
    sizes = [block] + [quarter] * 6
    waits = [(0, 1, 2), (3,), (4,), (), (5,), (6,), ()]
    at = 0
    for size, wait in zip(sizes, waits):
        yield at, size, wait
        at += size


def head_kernel(c, starts, off_ref, n_hbm, wq, wk, wv, a, far, ya, yfar, hcot_hbm, *refs):
    d_ref, dn_ref, w_ref, n_ref, h_ref, qkv_ref, sems = refs[-7:]
    rows = n_ref.shape[0]
    qw = GROUP * HD
    first = fetch([(n_hbm, n_ref, sems.at[7])])[0]
    copies = fetch(weight_copies((wq, wk, wv, a, far, ya, yfar), starts, c, w_ref, sems))
    cots = fetch([(hcot_hbm.at[:, c * qw : (c + 1) * qw], h_ref, sems.at[8])])[0]
    first.wait()
    total = None
    for i, (start, count, waits) in enumerate(piece_rows(wq.shape[0])):
        for k in waits:
            copies[k].wait()
        at = pl.ds(pl.multiple_of(off_ref[i], 128), count)
        part = jnp.dot(
            n_ref[:, at], w_ref[start : start + count, :], preferred_element_type=jnp.float32
        )
        total = part if total is None else total + part
    qkv_ref[...] = total.astype(jnp.bfloat16)
    cots.wait()
    mem = rows - (rows // 128) * 128
    seg_len = rows - mem
    keys = jnp.concatenate([qkv_ref[:, qw : qw + HD], qkv_ref[seg_len:, qw : qw + HD]], 0)
    values = jnp.concatenate([qkv_ref[:, qw + HD :], qkv_ref[seg_len:, qw + HD :]], 0)
    scale = HD ** (-0.5)
    wide = rows + mem
    row = lax.broadcasted_iota(jnp.int32, (rows, wide), 0)
    col = lax.broadcasted_iota(jnp.int32, (rows, wide), 1)
    need = jnp.where(col < seg_len, col, jnp.where(col < rows, 0, col - mem))
    seen = row >= need
    d_keys = None
    d_values = None
    for g in range(GROUP):
        q = qkv_ref[:, g * HD : (g + 1) * HD]
        da = h_ref[:, g * HD : (g + 1) * HD]
        s = jnp.where(seen, times_t(q, keys) * scale, -1e30)
        e = jnp.exp(s - jnp.max(s, -1, keepdims=True))
        p = e / jnp.sum(e, -1, keepdims=True)
        dp = times_t(da, values)
        ds = (p * (dp - jnp.sum(p * dp, -1, keepdims=True)) * scale).astype(jnp.bfloat16)
        d_ref[:, g * HD : (g + 1) * HD] = jnp.dot(
            ds, keys, preferred_element_type=jnp.float32
        ).astype(jnp.bfloat16)
        dk = inner_rows(ds, q)
        dv = inner_rows(p.astype(jnp.bfloat16), da)
        d_keys = dk if d_keys is None else d_keys + dk
        d_values = dv if d_values is None else d_values + dv
    for at, both in ((qw, d_keys), (qw + HD, d_values)):
        d_ref[:seg_len, at : at + HD] = both[:seg_len].astype(jnp.bfloat16)
        d_ref[seg_len:, at : at + HD] = (both[seg_len:rows] + both[rows:]).astype(jnp.bfloat16)
    for i, (start, count, _) in enumerate(piece_rows(wq.shape[0])):
        at = pl.ds(pl.multiple_of(off_ref[i], 128), count)
        part = times_t(d_ref[...], w_ref[start : start + count, :])
        dn_ref[:, at] = refs[0][:, at] + part if len(refs) > 7 else part


def rows_kernel(dn_ref, tok_ref, mem_ref, gain_ref, cot_ref, token0, token1, memory_ref, gg_ref):
    seg_len = tok_ref.shape[0]
    gain = gain_ref[...].astype(jnp.float32)
    step = mem_ref.shape[0]

    def piece(rows, dn, cot):
        zf = rows.astype(jnp.float32)
        inv = lax.rsqrt(jnp.mean(zf * zf, -1, keepdims=True) + 1e-05)
        unit = zf * inv
        gg_ref[...] += jnp.sum(dn * unit, 0, keepdims=True)
        du = dn * gain
        out = cot.astype(jnp.float32) + inv * (
            du - unit * jnp.mean(du * unit, -1, keepdims=True)
        )
        return out.astype(jnp.bfloat16)

    gg_ref[...] = jnp.zeros_like(gg_ref)

    for k, token_ref in enumerate((token0, token1)):

        @pl.loop(0, seg_len // 2 // step)
        def _(i, token_ref=token_ref, k=k):
            to = pl.ds(pl.multiple_of(i * step, step), step)
            at = pl.ds(pl.multiple_of(k * seg_len // 2 + i * step, step), step)
            token_ref[to, :] = piece(tok_ref[at, :], dn_ref[at, :], cot_ref[at, :])

    memory_ref[...] = piece(mem_ref[...], dn_ref[seg_len:, :], cot_ref[seg_len:, :])


def turn_kernel(n0, n1, n2, n3, out_ref, cat_ref, sems):
    rows = n0.shape[0]
    copies = fetch(
        [
            (ref, cat_ref.at[i * rows : (i + 1) * rows, :], sems.at[i])
            for i, ref in enumerate((n0, n1, n2, n3))
        ]
    )
    for copy in copies:
        copy.wait()
    for i in range(out_ref.shape[0] // 256):
        at = slice(256 * i, 256 * (i + 1))
        out_ref[at, :] = cat_ref[:, at].T


def grads_kernel(first, count, own, place_ref, nt_ref, d0, d1, d2, d3, *refs):
    dcat_ref = refs[-1]
    outs = refs[-4 - (count > 0) : -1] if own else refs[-2:-1]

    @pl.when(place_ref[5] == 1)
    def _():
        rows = d0.shape[0]
        for i, ref in enumerate((d0, d1, d2, d3)):
            dcat_ref[i * rows : (i + 1) * rows, :] = ref[...]
        block = nt_ref.shape[0] // 2
        qw = GROUP * HD
        if count:
            other = pl.ds(pl.multiple_of(place_ref[2] + first, 128), count)
            outs[0][...] = jnp.dot(
                nt_ref[other, :], dcat_ref[...], preferred_element_type=jnp.float32
            ).astype(jnp.bfloat16)
        if own:
            mine = pl.ds(pl.multiple_of(place_ref[3], 128), block)
            q_ref, k_ref, v_ref = outs[-3:]
            total = jnp.dot(nt_ref[mine, :], dcat_ref[...], preferred_element_type=jnp.float32)
            q_ref[...] = total[:, :qw]
            k_ref[...] = total[:, qw : qw + HD]
            v_ref[...] = total[:, qw + HD :]


def place_kernel(spots, place_ref, *refs):
    recvs = refs[: len(spots)]
    q_ref, k_ref, v_ref, q_buf, k_buf, v_buf, sems = refs[len(spots) + 3 : len(spots) + 10]
    held = refs[len(spots) + 10 :]
    qw = GROUP * HD

    @pl.when(place_ref[5] == 0)
    def _():
        waiting = []
        if held:
            coming = fetch([(recv, held[0].at[n], held[1].at[n]) for n, recv in enumerate(recvs)])
        for n, ((c, first), recv) in enumerate(zip(spots, recvs)):
            count = recv.shape[0]
            if held:
                coming[n].wait()
                recv = held[0].at[n]
            for k, (buf, ref, at, wide) in enumerate(
                ((q_buf, q_ref, 0, qw), (k_buf, k_ref, qw, HD), (v_buf, v_ref, qw + HD, HD))
            ):
                buf[n, :count, :] = recv[:, at : at + wide].astype(jnp.float32)
                copy = pltpu.make_async_copy(
                    buf.at[n, :count, :],
                    ref.at[first : first + count, c * wide : (c + 1) * wide],
                    sems.at[n, k],
                )
                copy.start()
                waiting.append(copy)
        for copy in waiting:
            copy.wait()


def copy_kernel(*refs):
    out_ref = refs[-1]
    at = 0
    for ref in refs[:-1]:
        out_ref[at : at + ref.shape[0], :] = ref[...]
        at += ref.shape[0]


class Order:
    def __init__(self, mark):
        self.mark = mark

    def point(self, *values):
        out = lax.optimization_barrier((self.mark,) + values)
        self.mark = out[0]
        return out[1] if len(values) == 1 else out[1:]


def on_line(inputs, memory, out_cot, head_cot, w_query, w_key, w_value, gain):
    tok = inputs[0, 0]
    mem = memory[0, 0]
    ocot = out_cot[0, 0]
    hcot = head_cot[0, 0]
    ws = (w_query[0], w_key[0], w_value[0])
    width = tok.shape[1]
    rows = tok.shape[0] + mem.shape[0]
    block = w_query.shape[1]
    quarter = block // 2
    qw = GROUP * HD
    cw = qw + 2 * HD
    z = lax.axis_index("seg")
    grp = lax.axis_index("grp")
    pair = z // 2
    inner = (z == 1) | (z == 2)
    partner = z + 1 - 2 * (z % 2)
    far_in = jnp.where(z < 2, 2, 1)
    far_out = jnp.where(z < 2, 3, 0)
    mine = grp * quarter
    theirs = (1 - grp) * quarter
    offsets = jnp.stack(
        [z * block]
        + [b * block + mine for b in (partner, far_out, far_in)]
        + [b * block + theirs for b in (partner, far_out, far_in)]
    ).astype(jnp.int32)
    places = jnp.stack(
        [
            pair * 2 * block,
            (1 - pair) * 2 * block,
            pair * block,
            (1 - pair) * block,
            grp,
            inner.astype(jnp.int32),
        ]
    ).astype(jnp.int32)

    smem = pl.BlockSpec(memory_space=pltpu.SMEM)
    vmem = pl.BlockSpec(memory_space=pltpu.VMEM)
    bf16 = jnp.bfloat16
    f32 = jnp.float32

    def shape(r, c, dtype=bf16):
        return jax.ShapeDtypeStruct((r, c), dtype)

    free = pl.CostEstimate(flops=0, bytes_accessed=0, transcendentals=0)
    anywhere = pl.BlockSpec(memory_space=pl.ANY)
    hbm = pl.BlockSpec(memory_space=pltpu.HBM)

    def part(r, c, at=0):
        return pl.BlockSpec((r, c), lambda *_: (0, at), pipeline_mode=pl.Buffered(1))

    def own_w(c):
        return [part(block, qw, c), part(block, HD, c), part(block, HD, c)]

    def call(kernel, outs, args, specs=None, mib=20, scratch=(), smems=1, aliases=None, out_specs=None):
        specs = specs or {}
        out_specs = out_specs or {}
        args = tuple(
            pltpu.with_memory_space_constraint(x, pltpu.HBM) if specs.get(k) is hbm else x
            for k, x in enumerate(args)
        )
        many = isinstance(outs, tuple)
        out_list = outs if many else (outs,)
        ins = [smem] * smems + [specs.get(k) or part(*args[k].shape) for k in range(smems, len(args))]
        ends = tuple(out_specs.get(k) or part(*o.shape) for k, o in enumerate(out_list))
        return pl.pallas_call(
            kernel,
            grid=(1,),
            out_shape=outs,
            in_specs=ins,
            out_specs=ends if many else ends[0],
            scratch_shapes=scratch,
            input_output_aliases=aliases or {},
            compiler_params=pltpu.CompilerParams(vmem_limit_bytes=mib * MIB),
            cost_estimate=free,
        )(*args)

    def permute(value, axis, route):
        return lax.ppermute(value, axis, route)

    def z_and(value):
        return jnp.concatenate(value, 0)

    order = Order(z.astype(jnp.int32))
    h01, h23 = call(
        halves_kernel,
        (shape(block, cw), shape(block, cw)),
        (places,) + ws,
        specs={k: hbm for k in (1, 2, 3)},
        scratch=[pltpu.SemaphoreType.DMA((12,))],
    )

    def head(i, pieces, starts, dn=()):
        args = (offsets, normed) + ws + tuple(pieces) + (hcot,)
        n = len(args)
        return call(
            functools.partial(head_kernel, i, starts),
            (shape(rows, cw), shape(rows, width, f32)),
            args + dn,
            specs={k: hbm for k in range(1, n)} | {6: anywhere},
            scratch=[
                pltpu.VMEM((width, cw), bf16),
                pltpu.VMEM((rows, width), bf16),
                pltpu.VMEM((rows, qw), bf16),
                pltpu.VMEM((rows, cw), bf16),
                pltpu.SemaphoreType.DMA((9,)),
            ],
            aliases={n: 1} if dn else None,
        )

    whole_shapes = tuple(shape(block, n * HEADS, f32) for n in (qw, HD, HD))

    def grads(i, n_t, ds, before, first=0, count=block, own=True):
        before = tuple(before) if own else ()
        args = (places, n_t) + tuple(ds) + before
        skip = 1 if count else 0
        outs = ((shape(count, cw),) if count else ()) + (whole_shapes if own else ())
        out = call(
            functools.partial(grads_kernel, first, count, own),
            outs,
            args,
            specs={6 + k: anywhere for k in range(len(before))},
            out_specs={skip + k: spec for k, spec in enumerate(own_w(i))} if own else None,
            scratch=[pltpu.VMEM((4 * rows, cw), bf16)],
            aliases={6 + k: skip + k for k in range(len(before))},
        )
        return (out[0] if count else None), out[skip:]

    def place(spots, recvs, before, from_hbm=False):
        n = 1 + len(spots)
        most = max(r.shape[0] for r in recvs)
        return call(
            functools.partial(place_kernel, spots),
            whole_shapes,
            (places,) + tuple(recvs) + tuple(before),
            specs={n + k: anywhere for k in range(3)}
            | ({1 + k: hbm for k in range(len(spots))} if from_hbm else {}),
            out_specs={k: anywhere for k in range(3)},
            scratch=[pltpu.VMEM((len(spots), most, w), f32) for w in (qw, HD, HD)]
            + [pltpu.SemaphoreType.DMA((len(spots), 3))]
            + (
                [
                    pltpu.VMEM((len(spots), most, cw), bf16),
                    pltpu.SemaphoreType.DMA((len(spots),)),
                ]
                if from_hbm
                else []
            ),
            aliases={n + k: k for k in range(3)},
        )

    def pick(b, c):
        return jnp.where(inner, b, c)

    def send(d):
        return [permute(d, "seg", r) for r in (INWARD, FAR_INWARD, ACROSS)]

    a01 = permute(h01, "seg", SWAP)
    normed, near, far = call(
        functools.partial(normalise_kernel, 2 * block),
        (shape(rows, width), shape(rows, 2 * block), shape(rows, 2 * block)),
        (places, tok, mem, gain),
    )
    n_across = permute(far, "seg", ACROSS)
    a01, n_across, h01, h23, normed, near, far = order.point(
        a01, n_across, h01, h23, normed, near, far
    )
    a23 = permute(h23, "seg", SWAP)
    b0 = permute(z_and([a01[:quarter], h01[:quarter]]), "seg", ACROSS)
    ya01 = permute(a01, "grp", GRPS)
    to1 = z_and([a01[quarter:], h01[quarter:]])
    n_far = permute(far, "seg", FAR_INWARD)
    b0, ya01, a23, to1, h23, near, n_far = order.point(b0, ya01, a23, to1, h23, near, n_far)
    ya23 = permute(a23, "grp", GRPS)
    b1 = permute(to1, "seg", ACROSS)
    c0 = permute(b0, "seg", OUTWARD)
    to2 = z_and([a23[:quarter], h23[:quarter]])
    to3 = z_and([a23[quarter:], h23[quarter:]])
    f0 = pick(b0, c0)
    ya23, b1, f0, to2, to3, near = order.point(ya23, b1, f0, to2, to3, near)
    yf0 = permute(f0, "grp", GRPS)
    n_in = permute(near, "seg", INWARD)
    b2 = permute(to2, "seg", ACROSS)
    c1 = permute(b1, "seg", OUTWARD)
    f1 = pick(b1, c1)
    n_in, b2, f1, to3 = order.point(n_in, b2, f1, to3)
    yf1 = permute(f1, "grp", GRPS)
    b3 = permute(to3, "seg", ACROSS)
    c2 = permute(b2, "seg", OUTWARD)
    d0, dn = head(0, (a01, f0, ya01, yf0), (0, 0))
    f2 = pick(b2, c2)
    b3, f2, d0, dn = order.point(b3, f2, d0, dn)
    yf2 = permute(f2, "grp", GRPS)
    c3 = permute(b3, "seg", OUTWARD)
    x0 = send(d0)
    d1, dn = head(1, (a01, f1, ya01, yf1), (quarter, quarter), (dn,))
    n_t = call(
        turn_kernel,
        shape(2 * block, 4 * rows),
        (near, n_in, n_far, n_across),
        specs={k: hbm for k in range(4)},
        scratch=[pltpu.VMEM((4 * rows, 2 * block), bf16), pltpu.SemaphoreType.DMA((4,))],
        smems=0,
    )
    f3 = pick(b3, c3)
    f3, x00, x01, x02, d1, dn, n_t = order.point(f3, *x0, d1, dn, n_t)
    yf3 = permute(f3, "grp", GRPS)
    x1 = send(d1)
    o0, whole = grads(0, n_t, (d0, x00, x01, x02), ())
    r0 = permute(o0, "seg", OUTWARD)
    d2, dn = head(2, (a23, f2, ya23, yf2), (0, 0), (dn,))
    x10, x11, x12, d2, dn, o0 = order.point(*x1, d2, dn, o0)
    x2 = send(d2)
    o1, whole = grads(1, n_t, (d1, x10, x11, x12), whole)
    r1 = permute(o1, "seg", OUTWARD)
    d3, dn = head(3, (a23, f3, ya23, yf3), (quarter, quarter), (dn,))
    x20, x21, x22, d3, r0, dn, o1 = order.point(*x2, d3, r0, dn, o1)
    x3 = send(d3)
    parts2 = (d2, x20, x21, x22)
    o2, _ = grads(2, n_t, parts2, (), own=False)
    r2 = permute(o2, "seg", OUTWARD)
    half_rows = tok.shape[0] // 2
    token0, token1, memory_part, grad_g = call(
        rows_kernel,
        (shape(half_rows, width), shape(half_rows, width), shape(mem.shape[0], width), shape(1, width, f32)),
        (dn, tok, mem, gain, ocot),
        smems=0,
    )
    gains = lax.all_to_all(grad_g.reshape(4, width // 4), "seg", 0, 0, tiled=True)
    x30, x31, x32, r1, r2, token0, token1, memory_part, gains = order.point(
        *x3, r1, r2, token0, token1, memory_part, gains
    )
    parts3 = (d3, x30, x31, x32)
    o3, _ = grads(3, n_t, parts3, (), own=False)
    r3 = permute(o3, "seg", OUTWARD)
    below0, before = deliver(token0, memory_part)
    below1 = from_behind(token1, "section", -1)
    _, whole = grads(2, n_t, parts2, whole, count=0)
    _, whole = grads(3, n_t, parts3, whole, count=0)
    grad_gain = jnp.sum(gains, 0, keepdims=True)
    whole = place(((0, 0), (1, 0), (2, 0)), (r0, r1, r2), whole, True)
    below = call(copy_kernel, shape(tok.shape[0], width), (below0, below1), smems=0)
    r3, before, below, grad_gain, q_, k_, v_ = order.point(r3, before, below, grad_gain, *whole)
    grad_query, grad_key, grad_value = place(((3, 0),), (r3,), (q_, k_, v_))
    return (
        below[None, None],
        before[None, None],
        grad_query[None],
        grad_key[None],
        grad_value[None],
        grad_gain,
    )


def solution(mesh):
    in_specs = (
        P("section", ("grp", "seg"), None, None),
        P("section", ("grp", "seg"), None, None),
        P("section", ("grp", "seg"), None, None),
        P("section", ("grp", "seg"), None, None),
        P("section", "seg", None),
        P("section", "seg", None),
        P("section", "seg", None),
        P("section", None),
    )
    out_specs = (
        P("section", ("grp", "seg"), None, None),
        P("section", ("grp", "seg"), None, None),
        P(("grp", "section"), "seg", None),
        P(("grp", "section"), "seg", None),
        P(("grp", "section"), "seg", None),
        P(("grp", "section"), "seg"),
    )
    line = mesh.shape["seg"] == 4 and mesh.shape["grp"] == 2
    return jax.shard_map(
        on_line if line else on_device,
        mesh=mesh,
        in_specs=in_specs,
        out_specs=out_specs,
        check_vma=False,
    )
```
